128 devices in a mesh: row: 8 (over x, core), col: 8 (over y, z_lo), seg: 2 (over z_hi).
Axes of the slice: x: 4, y: 4, z: 4 (z_hi: 2, z_lo: 2; z = z_hi * 2 + z_lo), core: 2. Of those that a mesh axis runs over, the one named last changes fastest.
Arguments:
- traces: float32 [64, 1024, 2000], P('seg', ('row', 'col')), may hold values from -100 to 100
- channel_alive: int32 [1024], P(('row', 'col')), may hold values 0 or 1
Outputs:
- stacks: float32 [1024, 1024, 401], P('row', ('col', 'seg'))
The draws below stay inside these ranges and needn't reach their ends.
All inputs are finite; a program needn't handle non-finite values. No bound on the sum of `channel_alive` on one device may be relied on, other than what follows from the above.
Results may differ from the reference program's by a relative error of at most 0.0028.
Values may be sent and summed in bfloat16 or wider, within the bound.
No kernel may reach another device: no remote copies, remote signals or barrier semaphores. Data moves between devices by JAX's collectives and lax.ppermute only.
A program may use at most 192 MiB of HBM per device.

```python
import math
import jax
import jax.numpy as jnp
from jax import lax

NT = 2000
NF = 192
F_LO = 8
MAXLAG = 200
SMOOTH = 5
CH_BLK = 128
CHANNELS = 1024
SEGMENTS = 64
N_ROW = 8


def draw_traces(key, part):
    key = jax.random.fold_in(key, 11)
    key_scale, key_noise = jax.random.split(key, 2)
    shape = (SEGMENTS, CHANNELS, NT)
    scales = jnp.exp(jax.random.uniform(key_scale, (1, CHANNELS, 1), jnp.float32, 0.0, math.log(10.0)))
    noise = jnp.clip(jax.random.normal(key_noise, shape, jnp.float32), -6.0, 6.0)
    colored = noise + 0.5 * jnp.roll(noise, 1, axis=-1)
    return scales * colored


def with_ends(drawn, rng, low, largest):
    index_at = [jax.random.randint(jax.random.fold_in(rng, axis), (), 0, length) for axis, length in enumerate(drawn.shape)]
    widest = drawn.shape.index(max(drawn.shape))
    beside = index_at[:widest] + [(index_at[widest] + 1) % drawn.shape[widest]] + index_at[widest + 1:]
    return drawn.at[tuple(index_at)].set(low).at[tuple(beside)].set(largest)


def setup_inputs(seed: int = 0) -> dict:
    keys = jax.random.split(jax.random.key(seed), 3)
    traces = draw_traces(jax.random.fold_in(keys[2], 71), 0)
    channel_alive = with_ends((jax.random.randint(keys[1], (CHANNELS,), 0, 8) < 7).astype(jnp.int32), jax.random.fold_in(keys[1], 1), 0, 1)
    return dict(traces=traces, channel_alive=channel_alive)


def whiten(real_part, imag_part, alive_mask):
    magnitude = jnp.sqrt(real_part * real_part + imag_part * imag_part)
    index_bins = jnp.arange(NF, dtype=jnp.int32)
    smoothing = (jnp.abs(index_bins[:, None] - index_bins[None, :]) <= SMOOTH).astype(jnp.float32)
    counts = lax.optimization_barrier(jnp.sum(smoothing, axis=0))
    smooth = jnp.dot(magnitude, smoothing, precision=lax.Precision.HIGHEST) / counts
    water_level = lax.optimization_barrier(jnp.mean(magnitude, axis=-1, keepdims=True))
    divisor = smooth + 0.05 * water_level + 1e-06
    weight = alive_mask.astype(jnp.float32)[None, :, None] / divisor
    white_real = (real_part * weight).astype(jnp.bfloat16)
    white_imag = (imag_part * weight).astype(jnp.bfloat16)
    return (white_real, white_imag)

def inverse_table():
    freqs = F_LO + jnp.arange(NF, dtype=jnp.int32)
    shifts = jnp.arange(2 * MAXLAG + 1, dtype=jnp.int32) - MAXLAG
    phase = jnp.mod(freqs[:, None] * shifts[None, :], NT).astype(jnp.float32) * (2.0 * math.pi / NT)
    scale_factor = 1.0 / math.sqrt(NF * SEGMENTS)
    return jnp.concatenate([jnp.cos(phase), jnp.sin(phase)], axis=0) * scale_factor

def reference(traces, channel_alive):
    times = jnp.arange(NT, dtype=jnp.int32).astype(jnp.float32)
    window_taper = 0.5 - 0.5 * jnp.cos((times + 0.5) * (2.0 * math.pi / NT))
    spectrum = jnp.fft.rfft(traces * window_taper, axis=-1)[..., F_LO:F_LO + NF]
    white_real, white_imag = whiten(jnp.real(spectrum), jnp.imag(spectrum), channel_alive)
    right_spec = jnp.concatenate([white_real, white_imag], axis=0).astype(jnp.float32)
    left_real = jnp.concatenate([white_real, white_imag], axis=0).astype(jnp.float32)
    left_imag = jnp.concatenate([white_imag, -white_real], axis=0).astype(jnp.float32)
    inv_table = inverse_table()
    left_real = left_real.reshape(2 * SEGMENTS, N_ROW, CH_BLK, NF).transpose(1, 0, 2, 3)
    left_imag = left_imag.reshape(2 * SEGMENTS, N_ROW, CH_BLK, NF).transpose(1, 0, 2, 3)

    def one_block(pair):
        block_real, block_imag = pair
        cross_real = jnp.einsum('sik,sjk->ijk', block_real, right_spec, precision=lax.Precision.HIGHEST)
        cross_imag = jnp.einsum('sik,sjk->ijk', block_imag, right_spec, precision=lax.Precision.HIGHEST)
        cross_all = jnp.concatenate([cross_real, cross_imag], axis=-1)
        return jnp.dot(cross_all, inv_table, precision=lax.Precision.HIGHEST)
    stacked = lax.map(one_block, (left_real, left_imag))
    return stacked.reshape(CHANNELS, CHANNELS, 2 * MAXLAG + 1)
```

```python
import functools
import math

import jax
import jax.numpy as jnp
import ml_dtypes
import numpy as np
from jax import lax
from jax.experimental import pallas as pl
from jax.experimental.pallas import tpu as pltpu
from jax.sharding import PartitionSpec as P

NT = 2000
NF = 192
F_LO = 8
MAXLAG = 200
LAGS = 2 * MAXLAG + 1
SMOOTH = 5
SEGS = 64
PAIRS = NF // 2
CH = 16
SEG_DEV = 32
AXES = ("row", "col", "seg")
XROWS = 104
LAG_ROWS = 416
VMEM = 60 * 2**20
BF16 = jnp.bfloat16
F32 = jnp.float32


def split_bf16(table, terms):
    rest = np.asarray(table, np.float64)
    parts = []
    for _ in range(terms):
        part = rest.astype(np.float32).astype(ml_dtypes.bfloat16)
        parts.append(part)
        rest = rest - part.astype(np.float64)
    return np.stack(parts)


def forward_table():
    times = np.arange(NT)
    window_taper = 0.5 - 0.5 * np.cos((times + 0.5) * (2.0 * np.pi / NT))
    rows = []
    for reim in range(2):
        for kpar in range(2):
            freqs = F_LO + 2 * np.arange(PAIRS) + kpar
            phase = np.mod(freqs[:, None] * times[None, :], NT) * (2.0 * np.pi / NT)
            wave = np.cos(phase) if reim == 0 else -np.sin(phase)
            rows.append(wave * window_taper[None, :])
    return np.concatenate(rows, axis=0)


def inverse_table():
    shifts = np.arange(LAGS) - MAXLAG
    cols = []
    for kpar in range(2):
        for reim in range(2):
            freqs = F_LO + 2 * np.arange(PAIRS) + kpar
            phase = np.mod(freqs[None, :] * shifts[:, None], NT) * (2.0 * np.pi / NT)
            cols.append(np.cos(phase) if reim == 0 else np.sin(phase))
    table = np.concatenate(cols, axis=1) / math.sqrt(NF * SEGS)
    table = np.concatenate([table, np.zeros((LAG_ROWS - LAGS, 2 * NF))], axis=0)
    return np.concatenate(list(split_bf16(table, 2)), axis=1)


def smoothing_tables():
    freqs = np.concatenate([2 * np.arange(PAIRS), 2 * np.arange(PAIRS) + 1])
    near = (np.abs(freqs[:, None] - freqs[None, :]) <= SMOOTH).astype(np.float32)
    return near.astype(ml_dtypes.bfloat16), near.sum(axis=1, keepdims=True)


def lane_tables():
    by_channel = np.zeros((512, 512), np.float32)
    by_group = np.zeros((512, 512), np.float32)
    seg, ch = np.meshgrid(np.arange(SEG_DEV), np.arange(CH), indexing="ij")
    by_channel[seg * CH + ch, ch * SEG_DEV + seg] = 1
    grp, sub, seg = np.meshgrid(np.arange(4), np.arange(4), np.arange(32), indexing="ij")
    by_group[grp * 128 + sub * 32 + seg, sub * 128 + grp * 32 + seg] = 1
    rows = np.zeros((128, 128), np.float32)
    ch, pair = np.meshgrid(np.arange(CH), np.arange(8), indexing="ij")
    rows[pair * CH + ch, ch * 8 + pair] = 1
    as16 = lambda t: t.astype(ml_dtypes.bfloat16)
    return as16(by_channel), as16(by_group), as16(rows)


def flat(x, y, z, core):
    return ((x * 2 + core) * 8 + (y * 2 + z % 2)) * 2 + z // 2


def places():
    return [
        (x, y, z, core)
        for x in range(4) for y in range(4) for z in range(4) for core in range(2)
    ]


def perm_of(move):
    return [(flat(*place), flat(*move(*place))) for place in places()]


def along_first(n):
    return perm_of(
        lambda x, y, z, core: (x, (y + n) % 4, z, core) if core == 0 else (x, y, (z + n) % 4, core)
    )


def along_second(n):
    return perm_of(
        lambda x, y, z, core: (x, (y + n) % 4, z, core) if core == 1 else (x, y, (z + n) % 4, core)
    )


def to_readers():
    return perm_of(
        lambda x, y, z, core: ((x + y + z) % 4, x, 2 * (y // 2) + core, y % 2)
    )


def slot_table():
    offsets, moves = (0, -1, 1, 2), (0, 1, -1, 2)
    table = np.zeros((128, 24), np.int32)
    for x, y, z, core in places():
        row = table[flat(x, y, z, core)]
        first, second = (y, z) if core == 0 else (z, y)
        for arr, n in enumerate(moves):
            for k in range(4):
                pos1, pos2 = (first + offsets[k]) % 4, (second - n) % 4
                ys, zs = (pos1, pos2) if core == 0 else (pos2, pos1)
                row[arr * 4 + k] = (2 * ys + zs % 2) * 2 + zs // 2
        for xs in range(4):
            for c2 in range(2):
                zs = (xs - y - (2 * (z // 2) + c2)) % 4
                row[16 + xs * 2 + c2] = (zs // 2) * 4 + c2 * 2 + zs % 2
    return table


def dot_nt(a, b):
    return lax.dot_general(a, b, (((1,), (1,)), ((), ())), preferred_element_type=F32)


def dot_nn(a, b):
    return jnp.dot(a, b, preferred_element_type=F32)


def split3(value):
    hi = value.astype(BF16)
    rest = value - hi.astype(F32)
    mid = rest.astype(BF16)
    return hi, mid, (rest - mid.astype(F32)).astype(BF16)


def spectra_kernel(
    alive_ref, traces_ref, table_ref, near_ref, counts_ref, chan_ref, group_ref, rows_ref,
    out_ref, white_ref,
):
    step = pl.program_id(0)
    segs = traces_ref.shape[0]
    lanes = segs * CH
    hi, mid, lo = split3(traces_ref[...].reshape(lanes, NT))
    t_hi, t_mid, t_lo = table_ref[0], table_ref[1], table_ref[2]
    spectra = dot_nt(t_lo, hi) + dot_nt(t_hi, lo) + dot_nt(t_mid, mid)
    spectra = spectra + (dot_nt(t_mid, hi) + dot_nt(t_hi, mid))
    spectra = spectra + dot_nt(t_hi, hi)
    real, imag = spectra[:NF], spectra[NF:]
    magnitude = jnp.sqrt(real * real + imag * imag)
    m_hi, m_mid, m_lo = split3(magnitude)
    near = near_ref[...]
    smooth = (dot_nn(near, m_lo) + dot_nn(near, m_mid) + dot_nn(near, m_hi)) / counts_ref[...]
    water = jnp.sum(magnitude, axis=0, keepdims=True) * (1.0 / NF)
    weight = 1.0 / (smooth + 0.05 * water + 1e-6)
    at = pl.ds(pl.multiple_of(step * lanes, 128), lanes)
    white_ref[:NF, at] = (real * weight).astype(BF16)
    white_ref[NF:, at] = (imag * weight).astype(BF16)

    @pl.when(step == pl.num_programs(0) - 1)
    def _():
        by_channel = dot_nn(white_ref[...], chan_ref[...]).astype(BF16)
        alive = [alive_ref[c].astype(F32) for c in range(CH)]
        grouped = []
        for b in range(4):
            lhs = jnp.concatenate(
                [by_channel[g * PAIRS:(g + 1) * PAIRS, 128 * b:128 * b + 128] for g in range(4)],
                axis=1,
            )
            grouped.append(dot_nn(lhs, group_ref[...]))
        for half in range(PAIRS // 16):
            cols = []
            for part in range(2):
                at8 = slice(16 * half + 8 * part, 16 * half + 8 * part + 8)
                cols.append(
                    jnp.concatenate(
                        [
                            grouped[c // 4][at8, 128 * (c % 4):128 * (c % 4) + 128] * alive[c]
                            for c in range(CH)
                        ],
                        axis=0,
                    )
                )
            block = jnp.concatenate(cols, axis=1).astype(BF16)
            block = dot_nn(rows_ref[...], block).astype(BF16)
            for part in range(2):
                at8 = slice(16 * half + 8 * part, 16 * half + 8 * part + 8)
                out_ref[at8] = block[:, 128 * part:128 * part + 128].reshape(8, CH, 128)


def whitened(traces, alive):
    steps = 2
    near, counts = smoothing_tables()
    by_channel, by_group, rows = lane_tables()
    table = split_bf16(forward_table(), 3)
    whole = lambda a: pl.BlockSpec(a.shape, lambda i: (0,) * a.ndim)
    consts = (table, near, counts, by_channel, by_group, rows)
    return pl.pallas_call(
        spectra_kernel,
        grid=(steps,),
        out_shape=jax.ShapeDtypeStruct((PAIRS, CH, 128), BF16),
        in_specs=[
            pl.BlockSpec(memory_space=pltpu.SMEM),
            pl.BlockSpec((SEG_DEV // steps, CH, NT), lambda i: (i, 0, 0)),
        ]
        + [whole(a) for a in consts],
        out_specs=pl.BlockSpec((PAIRS, CH, 128), lambda i: (0, 0, 0)),
        scratch_shapes=[pltpu.VMEM((2 * NF, SEG_DEV * CH), BF16)],
        compiler_params=pltpu.CompilerParams(vmem_limit_bytes=VMEM),
        name="whitened_spectra",
    )(alive, traces, *(jnp.asarray(a) for a in consts))


CHUNKS = 4
PER = PAIRS // CHUNKS
J_STEP = 8


def stack_kernel(slots_ref, *refs):
    parts, second_ref, table_ref, out_ref = refs[:4], refs[4], refs[5], refs[6]
    left, right = refs[7:9]
    cross_refs, sems = refs[9:13], refs[13]
    step = pl.program_id(0)

    def copies(chunk):
        at = pl.ds(chunk * PER, PER)
        found = []
        for n in range(8):
            slot = slots_ref[16 + n]
            found.append((second_ref.at[n, at], right.at[slot, at]))
        for arr, ref in enumerate(parts):
            for k in range(4):
                found.append((ref.at[k, at], left.at[slots_ref[arr * 4 + k], at]))
        return [
            pltpu.make_async_copy(src, dst, sems.at[chunk, n])
            for n, (src, dst) in enumerate(found)
        ]

    @pl.when(step == 0)
    def _():
        pending = [copies(chunk) for chunk in range(CHUNKS)]
        for chunk in pending:
            for copy in chunk:
                copy.start()
        lane = lax.broadcasted_iota(jnp.int32, (CH, 128), 1)
        even = (lane // 32) % 2 == 0
        one, zero = jnp.float32(1), jnp.float32(0)
        sign = jnp.where(lane < 64, -one, one)
        keep0 = jnp.where(even, one, zero).astype(BF16)
        keep1 = jnp.where(even, zero, one).astype(BF16)
        turn0 = (sign * jnp.where(even, one, zero)).astype(BF16)
        turn1 = (sign * jnp.where(even, zero, one)).astype(BF16)

        def cross(p, _):
            first = jnp.concatenate(
                [jnp.concatenate([left[2 * u + h, p] for u in range(8)], axis=0) for h in range(2)],
                axis=1,
            )
            cols = []
            for h in range(2):
                blocks = [right[4 * h + n, p] for n in range(4)]
                swapped = [jnp.concatenate([b[:, 64:], b[:, :64]], axis=1) for b in blocks]
                cols.append(
                    jnp.concatenate(
                        [b * keep0 for b in blocks]
                        + [b * turn0 for b in swapped]
                        + [b * keep1 for b in blocks]
                        + [b * turn1 for b in swapped],
                        axis=0,
                    )
                )
            product = dot_nt(jnp.concatenate(cols, axis=1), first)
            for g in range(4):
                cross_refs[g][pl.ds(p, 64, stride=XROWS), :] = product[64 * g:64 * g + 64]
            return 0

        for chunk in range(CHUNKS):
            for copy in pending[chunk]:
                copy.wait()
            lax.fori_loop(chunk * PER, (chunk + 1) * PER, cross, 0, unroll=UNROLL)

    table = table_ref[...]
    out_rows = out_ref.reshape(LAGS * J_STEP, 128)
    for pair in range(J_STEP // 2):
        cols = []
        for e in range(2):
            j = step * J_STEP + 2 * pair + e
            at = pl.ds(pl.multiple_of(j * XROWS, 8), PAIRS)
            cols.append(jnp.concatenate([ref[at, :].astype(BF16) for ref in cross_refs], axis=0))
        both = jnp.concatenate(cols, axis=1)
        lags = dot_nn(table, jnp.concatenate([both, both], axis=0))
        for e in range(2):
            out_rows[pl.ds(2 * pair + e, LAGS, stride=J_STEP), :] = lags[:LAGS, 128 * e:128 * e + 128]


UNROLL = 12


def stacked(slots, parts, second, table):
    any_spec = pl.BlockSpec(memory_space=pl.ANY)
    return pl.pallas_call(
        stack_kernel,
        grid_spec=pltpu.PrefetchScalarGridSpec(
            num_scalar_prefetch=1,
            grid=(64 // J_STEP,),
            in_specs=[any_spec] * 5 + [pl.BlockSpec(table.shape, lambda u, s: (0, 0))],
            out_specs=pl.BlockSpec((LAGS, J_STEP, 128), lambda u, s: (0, u, 0)),
            scratch_shapes=[
                pltpu.VMEM((16, PAIRS, CH, 128), BF16),
                pltpu.VMEM((8, PAIRS, CH, 128), BF16),
            ]
            + [pltpu.VMEM((64 * XROWS, 128), F32)] * 4
            + [pltpu.SemaphoreType.DMA((CHUNKS, 24))],
        ),
        out_shape=jax.ShapeDtypeStruct((LAGS, 64, 128), F32),
        compiler_params=pltpu.CompilerParams(vmem_limit_bytes=VMEM),
        cost_estimate=pl.CostEstimate(
            flops=2 * 10**10, bytes_accessed=24 * 2**20, transcendentals=0
        ),
        name="stacks",
    )(slots, *parts, second, table)


def body(traces, channel_alive):
    own = whitened(traces, channel_alive)
    device = (lax.axis_index("row") * 8 + lax.axis_index("col")) * 2 + lax.axis_index("seg")
    slots = lax.dynamic_index_in_dim(jnp.asarray(slot_table()), device, 0, keepdims=False)
    send = lambda a, perm: lax.ppermute(a, AXES, perm)
    first = [own] + [send(own, along_first(n)) for n in (1, -1, 2)]
    second = send(own, to_readers())
    *first, second = lax.optimization_barrier((*first, second))
    mine = jnp.stack(first)
    second = lax.all_gather(second, "row", axis=0)
    parts = [mine] + [send(mine, along_second(n)) for n in (1, -1, 2)]
    out = stacked(slots, parts, second, jnp.asarray(inverse_table()))
    return jnp.transpose(out, (2, 1, 0))


def solution(mesh):
    return jax.shard_map(
        body,
        mesh=mesh,
        in_specs=(P("seg", ("row", "col"), None), P(("row", "col"))),
        out_specs=P("row", ("col", "seg"), None),
        check_vma=False,
    )
```

```python
import functools
import math

import jax
import jax.numpy as jnp
import ml_dtypes
import numpy as np
from jax import lax
from jax.experimental import pallas as pl
from jax.experimental.pallas import tpu as pltpu
from jax.sharding import PartitionSpec as P

NT = 2000
NF = 192
F_LO = 8
MAXLAG = 200
LAGS = 2 * MAXLAG + 1
SMOOTH = 5
SEGS = 64
PAIRS = NF // 2
CH = 16
SEG_DEV = 32
AXES = ("row", "col", "seg")
XROWS = 104
LAG_ROWS = 208
TERMS = 2
VMEM = 60 * 2**20
BF16 = jnp.bfloat16
F32 = jnp.float32


def split_bf16(table, terms):
    rest = np.asarray(table, np.float64)
    parts = []
    for _ in range(terms):
        part = rest.astype(np.float32).astype(ml_dtypes.bfloat16)
        parts.append(part)
        rest = rest - part.astype(np.float64)
    return np.stack(parts)


def forward_table():
    times = np.arange(NT)
    window_taper = 0.5 - 0.5 * np.cos((times + 0.5) * (2.0 * np.pi / NT))
    rows = []
    for reim in range(2):
        for kpar in range(2):
            freqs = F_LO + 2 * np.arange(PAIRS) + kpar
            phase = np.mod(freqs[:, None] * times[None, :], NT) * (2.0 * np.pi / NT)
            wave = np.cos(phase) if reim == 0 else -np.sin(phase)
            rows.append(wave * window_taper[None, :])
    return np.concatenate(rows, axis=0)


def inverse_table():
    shifts = np.arange(LAG_ROWS)
    parts = []
    for reim in range(2):
        cols = []
        for kpar in range(2):
            freqs = F_LO + 2 * np.arange(PAIRS) + kpar
            phase = np.mod(freqs[None, :] * shifts[:, None], NT) * (2.0 * np.pi / NT)
            cols.append(np.cos(phase) if reim == 0 else np.sin(phase))
        table = np.concatenate(cols, axis=1) / math.sqrt(NF * SEGS)
        parts.append(np.concatenate(list(split_bf16(table, TERMS)), axis=1))
    return np.concatenate(parts, axis=0)


def smoothing_tables():
    freqs = np.concatenate([2 * np.arange(PAIRS), 2 * np.arange(PAIRS) + 1])
    near = (np.abs(freqs[:, None] - freqs[None, :]) <= SMOOTH).astype(np.float32)
    return near.astype(ml_dtypes.bfloat16), near.sum(axis=1, keepdims=True)


def lane_tables():
    by_channel = np.zeros((512, 512), np.float32)
    by_group = np.zeros((512, 512), np.float32)
    seg, ch = np.meshgrid(np.arange(SEG_DEV), np.arange(CH), indexing="ij")
    by_channel[seg * CH + ch, ch * SEG_DEV + seg] = 1
    grp, sub, seg = np.meshgrid(np.arange(4), np.arange(4), np.arange(32), indexing="ij")
    by_group[grp * 128 + sub * 32 + seg, sub * 128 + grp * 32 + seg] = 1
    rows = np.zeros((128, 128), np.float32)
    ch, pair = np.meshgrid(np.arange(CH), np.arange(8), indexing="ij")
    rows[pair * CH + ch, ch * 8 + pair] = 1
    as16 = lambda t: t.astype(ml_dtypes.bfloat16)
    return as16(by_channel), as16(by_group), as16(rows)


def flat(x, y, z, core):
    return ((x * 2 + core) * 8 + (y * 2 + z % 2)) * 2 + z // 2


def places():
    return [
        (x, y, z, core)
        for x in range(4) for y in range(4) for z in range(4) for core in range(2)
    ]


def perm_of(move):
    return [(flat(*place), flat(*move(*place))) for place in places()]


def along_first(n):
    return perm_of(
        lambda x, y, z, core: (x, (y + n) % 4, z, core) if core == 0 else (x, y, (z + n) % 4, core)
    )


def along_second(n):
    return perm_of(
        lambda x, y, z, core: (x, (y + n) % 4, z, core) if core == 1 else (x, y, (z + n) % 4, core)
    )


def to_readers():
    return perm_of(
        lambda x, y, z, core: ((x + y + z + 2 * core) % 4, x, 2 * (y // 2) + core, y % 2)
    )


def along_x(n):
    return perm_of(lambda x, y, z, core: ((x + n) % 4, y, z, core))


def other_core():
    return perm_of(lambda x, y, z, core: (x, y, z, 1 - core))


def slot_table():
    offsets = (0, -1, 1, 2)
    first_order = [(k, n) for n in (0, 1, -1) for k in range(4)] + [(k, 2) for k in range(4)]
    table = np.zeros((128, 24), np.int32)
    for x, y, z, core in places():
        row = table[flat(x, y, z, core)]
        first, second = (y, z) if core == 0 else (z, y)
        for at, (k, n) in enumerate(first_order):
            pos1, pos2 = (first + offsets[k]) % 4, (second - n) % 4
            ys, zs = (pos1, pos2) if core == 0 else (pos2, pos1)
            row[at] = (2 * ys + zs % 2) * 2 + zs // 2
        for other in range(2):
            for k in range(4):
                c2 = core ^ other
                ys, xs = 2 * (z // 2) + c2, (x + offsets[k]) % 4
                zs = (xs - y - ys - 2 * (z % 2)) % 4
                row[16 + other * 4 + k] = (zs // 2) * 4 + c2 * 2 + zs % 2
    return table


def dot_nt(a, b):
    return lax.dot_general(a, b, (((1,), (1,)), ((), ())), preferred_element_type=F32)


def dot_nn(a, b):
    return jnp.dot(a, b, preferred_element_type=F32)


def split3(value):
    hi = value.astype(BF16)
    rest = value - hi.astype(F32)
    mid = rest.astype(BF16)
    return hi, mid, (rest - mid.astype(F32)).astype(BF16)


def spectra_kernel(
    alive_ref, traces_ref, table_ref, near_ref, counts_ref, chan_ref, group_ref, rows_ref,
    out_ref, total_ref,
):
    step = pl.program_id(0)
    lanes = SEG_DEV * CH
    width = traces_ref.shape[2]
    traces = traces_ref[...].reshape(lanes, width)
    inside = lax.broadcasted_iota(jnp.int32, (1, width), 1) < NT - step * width
    hi, mid, lo = split3(jnp.where(inside, traces, 0.0))
    rows = 2 * NF
    by_hi = dot_nt(table_ref[...], hi)
    by_mid = dot_nt(table_ref[: 2 * rows], mid)
    by_lo = dot_nt(table_ref[:rows], lo)
    small = by_hi[2 * rows :] + by_lo + by_mid[rows:]
    added = by_hi[:rows] + (by_hi[rows : 2 * rows] + by_mid[:rows] + small)

    @pl.when(step == 0)
    def _():
        total_ref[...] = added

    @pl.when(step > 0)
    def _():
        total_ref[...] += added

    @pl.when(step == pl.num_programs(0) - 1)
    def _():
        real, imag = total_ref[:NF], total_ref[NF:]
        magnitude = jnp.sqrt(real * real + imag * imag)
        m_hi, m_mid, m_lo = split3(magnitude)
        near = near_ref[...]
        smooth = (dot_nn(near, m_lo) + dot_nn(near, m_mid) + dot_nn(near, m_hi)) / counts_ref[...]
        water = jnp.sum(magnitude, axis=0, keepdims=True) * (1.0 / NF)
        weight = 1.0 / (smooth + 0.05 * water + 1e-6)
        white = jnp.concatenate([real * weight, imag * weight], axis=0).astype(BF16)
        by_channel = dot_nn(white, chan_ref[...]).astype(BF16)
        alive = [alive_ref[c].astype(F32) for c in range(CH)]
        lhs = jnp.concatenate(
            [
                jnp.concatenate(
                    [by_channel[g * PAIRS:(g + 1) * PAIRS, 128 * b:128 * b + 128] for g in range(4)],
                    axis=1,
                )
                for b in range(4)
            ],
            axis=0,
        )
        grouped = dot_nn(lhs, group_ref[...])
        for half in range(PAIRS // 16):
            cols = []
            for part in range(2):
                at = 16 * half + 8 * part
                cols.append(
                    jnp.concatenate(
                        [
                            grouped[
                                PAIRS * (c // 4) + at:PAIRS * (c // 4) + at + 8,
                                128 * (c % 4):128 * (c % 4) + 128,
                            ]
                            * alive[c]
                            for c in range(CH)
                        ],
                        axis=0,
                    )
                )
            block = jnp.concatenate(cols, axis=1).astype(BF16)
            block = dot_nn(rows_ref[...], block).astype(BF16)
            for part in range(2):
                at = 16 * half + 8 * part
                out_ref[at:at + 8] = block[:, 128 * part:128 * part + 128].reshape(8, CH, 128)


def whitened(traces, alive):
    width = 512
    near, counts = smoothing_tables()
    by_channel, by_group, rows = lane_tables()
    table = split_bf16(forward_table(), 3).reshape(6 * NF, NT)
    table = np.concatenate([table, np.zeros((6 * NF, 4 * width - NT), table.dtype)], axis=1)
    whole = lambda a: pl.BlockSpec(a.shape, lambda i: (0,) * a.ndim)
    consts = (near, counts, by_channel, by_group, rows)
    return pl.pallas_call(
        spectra_kernel,
        grid=(4,),
        out_shape=jax.ShapeDtypeStruct((PAIRS, CH, 128), BF16),
        in_specs=[
            pl.BlockSpec(memory_space=pltpu.SMEM),
            pl.BlockSpec((SEG_DEV, CH, width), lambda i: (0, 0, i)),
            pl.BlockSpec((6 * NF, width), lambda i: (0, i)),
        ]
        + [whole(a) for a in consts],
        out_specs=pl.BlockSpec((PAIRS, CH, 128), lambda i: (0, 0, 0)),
        scratch_shapes=[pltpu.VMEM((2 * NF, SEG_DEV * CH), F32)],
        compiler_params=pltpu.CompilerParams(vmem_limit_bytes=VMEM),
        name="whitened_spectra",
    )(alive, traces, *(jnp.asarray(a) for a in (table,) + consts))


CHUNKS = 4
PER = PAIRS // CHUNKS
J_STEP = 8


def stack_kernel(slots_ref, *refs):
    sources, table_ref, out_ref = refs[:7], refs[7], refs[8]
    left, right = refs[9:11]
    cross_refs, sems = refs[11:15], refs[15]
    step = pl.program_id(0)

    def copies(chunk):
        at = pl.ds(chunk * PER, PER)
        found = []
        for ref in sources:
            for k in range(ref.shape[0]):
                to = left if len(found) < 16 else right
                found.append((ref.at[k, at], to.at[slots_ref[len(found)], at]))
        return [
            pltpu.make_async_copy(src, dst, sems.at[chunk, n])
            for n, (src, dst) in enumerate(found)
        ]

    @pl.when(step == 0)
    def _():
        pending = [copies(chunk) for chunk in range(CHUNKS)]
        for chunk in pending:
            for copy in chunk:
                copy.start()
        lane = lax.broadcasted_iota(jnp.int32, (CH, 128), 1)
        even = (lane // 32) % 2 == 0
        one, zero = jnp.float32(1), jnp.float32(0)
        sign = jnp.where(lane < 64, -one, one)
        keep0 = jnp.where(even, one, zero).astype(BF16)
        keep1 = jnp.where(even, zero, one).astype(BF16)
        turn0 = (sign * jnp.where(even, one, zero)).astype(BF16)
        turn1 = (sign * jnp.where(even, zero, one)).astype(BF16)

        def cross(p, _):
            first = jnp.concatenate(
                [jnp.concatenate([left[2 * u + h, p] for u in range(8)], axis=0) for h in range(2)],
                axis=1,
            )
            cols = []
            for h in range(2):
                blocks = [right[4 * h + n, p] for n in range(4)]
                swapped = [jnp.concatenate([b[:, 64:], b[:, :64]], axis=1) for b in blocks]
                cols.append(
                    jnp.concatenate(
                        [b * keep0 for b in blocks]
                        + [b * turn0 for b in swapped]
                        + [b * keep1 for b in blocks]
                        + [b * turn1 for b in swapped],
                        axis=0,
                    )
                )
            product = dot_nt(jnp.concatenate(cols, axis=1), first)
            for g in range(4):
                cross_refs[g][pl.ds(p, 64, stride=XROWS), :] = product[64 * g:64 * g + 64]
            return 0

        for chunk in range(CHUNKS):
            for copy in pending[chunk]:
                copy.wait()
            lax.fori_loop(chunk * PER, (chunk + 1) * PER, cross, 0, unroll=UNROLL)

    out_rows = out_ref.reshape(LAGS * J_STEP, 128)
    turned = 7 - lax.broadcasted_iota(jnp.int32, (LAG_ROWS // 8, 8, 128), 1)
    for pair in range(J_STEP // 2):
        halves = []
        for reim in range(2):
            cols = []
            for e in range(2):
                j = step * J_STEP + 2 * pair + e
                at = pl.ds(pl.multiple_of(j * XROWS, 8), PAIRS)
                x = [cross_refs[2 * kpar + reim][at, :].astype(BF16) for kpar in range(2)]
                cols.append(jnp.concatenate(x * TERMS, axis=0))
            rows = slice(LAG_ROWS * reim, LAG_ROWS * (reim + 1))
            halves.append(dot_nn(table_ref[rows, :], jnp.concatenate(cols, axis=1)))
        later, earlier = halves[0] + halves[1], halves[0] - halves[1]
        for e in range(2):
            lanes, j = slice(128 * e, 128 * e + 128), 2 * pair + e
            back = earlier[:, lanes].reshape(LAG_ROWS // 8, 8, 128)
            back = jnp.take_along_axis(back, turned, axis=1)
            for v in range(MAXLAG // 8):
                out_rows[pl.ds((MAXLAG - 7 - 8 * v) * J_STEP + j, 8, stride=J_STEP), :] = back[v]
            out_rows[pl.ds(j, 1), :] = earlier[MAXLAG:MAXLAG + 1, lanes]
            out_rows[pl.ds(MAXLAG * J_STEP + j, MAXLAG + 1, stride=J_STEP), :] = later[: MAXLAG + 1, lanes]


UNROLL = 24


def stacked(slots, sources, table):
    any_spec = pl.BlockSpec(memory_space=pl.ANY)
    return pl.pallas_call(
        stack_kernel,
        grid_spec=pltpu.PrefetchScalarGridSpec(
            num_scalar_prefetch=1,
            grid=(64 // J_STEP,),
            in_specs=[any_spec] * len(sources) + [pl.BlockSpec(table.shape, lambda u, s: (0, 0))],
            out_specs=pl.BlockSpec((LAGS, J_STEP, 128), lambda u, s: (0, u, 0)),
            scratch_shapes=[
                pltpu.VMEM((16, PAIRS, CH, 128), BF16),
                pltpu.VMEM((8, PAIRS, CH, 128), BF16),
            ]
            + [pltpu.VMEM((64 * XROWS, 128), F32)] * 4
            + [pltpu.SemaphoreType.DMA((CHUNKS, 24))],
        ),
        out_shape=jax.ShapeDtypeStruct((LAGS, 64, 128), F32),
        compiler_params=pltpu.CompilerParams(vmem_limit_bytes=VMEM),
        cost_estimate=pl.CostEstimate(
            flops=2 * 10**10, bytes_accessed=24 * 2**20, transcendentals=0
        ),
        name="stacks",
    )(slots, *sources, table)


def body(traces, channel_alive):
    own = whitened(traces, channel_alive)
    device = (lax.axis_index("row") * 8 + lax.axis_index("col")) * 2 + lax.axis_index("seg")
    slots = lax.dynamic_index_in_dim(jnp.asarray(slot_table()), device, 0, keepdims=False)
    send = lambda a, perm: lax.ppermute(a, AXES, perm)
    first = [own] + [send(own, along_first(n)) for n in (1, -1, 2)]
    second = send(own, to_readers())
    *first, second = lax.optimization_barrier((*first, second))
    mine = jnp.stack(first)
    up, down = send(mine, along_second(1)), send(mine, along_second(-1))
    seconds = [second] + [send(second, along_x(n)) for n in (1, -1, 2)]
    up, down, *seconds = lax.optimization_barrier((up, down, *seconds))
    seconds = jnp.stack(seconds)
    far_up, far_down = send(up[:2], along_second(1)), send(down[2:], along_second(-1))
    others = send(seconds, other_core())
    sources = (mine, up, down, far_up, far_down, seconds, others)
    out = stacked(slots, sources, jnp.asarray(inverse_table()))
    return jnp.transpose(out, (2, 1, 0))


def solution(mesh):
    return jax.shard_map(
        body,
        mesh=mesh,
        in_specs=(P("seg", ("row", "col"), None), P(("row", "col"))),
        out_specs=P("row", ("col", "seg"), None),
        check_vma=False,
    )
```

```python
import functools
import math

import jax
import jax.numpy as jnp
import ml_dtypes
import numpy as np
from jax import lax
from jax.experimental import pallas as pl
from jax.experimental.pallas import tpu as pltpu
from jax.sharding import PartitionSpec as P

NT = 2000
NF = 192
F_LO = 8
MAXLAG = 200
LAGS = 2 * MAXLAG + 1
SMOOTH = 5
SEGS = 64
PAIRS = NF // 2
HALF = 1024
CH = 16
SEG_DEV = 32
AXES = ("row", "col", "seg")
XROWS = 104
LAG_ROWS = 208
TERMS = 2
VMEM = 60 * 2**20
BF16 = jnp.bfloat16
F32 = jnp.float32


def split_bf16(table, terms):
    rest = np.asarray(table, np.float64)
    parts = []
    for _ in range(terms):
        part = rest.astype(np.float32).astype(ml_dtypes.bfloat16)
        parts.append(part)
        rest = rest - part.astype(np.float64)
    return np.stack(parts)


def forward_tables():
    times = np.arange(HALF) + 0.5
    window_taper = (0.5 - 0.5 * np.cos(times * (2.0 * np.pi / NT))) * (np.arange(HALF) < NT // 2)
    freqs = F_LO + np.concatenate([2 * np.arange(PAIRS), 2 * np.arange(PAIRS) + 1])
    phase = np.mod(freqs[:, None] * times[None, :], NT) * (2.0 * np.pi / NT)
    waves = [split_bf16(wave * window_taper, 3) for wave in (np.cos(phase), np.sin(phase))]
    table = np.concatenate([wave.reshape(3 * NF, HALF) for wave in waves], axis=0)
    angle = freqs[:, None] * (np.pi / NT)
    turn = np.concatenate([np.cos(angle), np.sin(angle)], axis=1).astype(np.float32)
    return table, turn


def inverse_table():
    shifts = np.arange(LAG_ROWS)
    parts = []
    for reim in range(2):
        cols = []
        for kpar in range(2):
            freqs = F_LO + 2 * np.arange(PAIRS) + kpar
            phase = np.mod(freqs[None, :] * shifts[:, None], NT) * (2.0 * np.pi / NT)
            cols.append(np.cos(phase) if reim == 0 else np.sin(phase))
        table = np.concatenate(cols, axis=1) / math.sqrt(NF * SEGS)
        parts.append(np.concatenate(list(split_bf16(table, TERMS)), axis=1))
    return np.concatenate(parts, axis=0)


def smoothing_tables():
    freqs = np.concatenate([2 * np.arange(PAIRS), 2 * np.arange(PAIRS) + 1])
    near = (np.abs(freqs[:, None] - freqs[None, :]) <= SMOOTH).astype(np.float32)
    return near.astype(ml_dtypes.bfloat16), near.sum(axis=1, keepdims=True)


def flat(x, y, z, core):
    return ((x * 2 + core) * 8 + (y * 2 + z % 2)) * 2 + z // 2


def places():
    return [
        (x, y, z, core)
        for x in range(4) for y in range(4) for z in range(4) for core in range(2)
    ]


def perm_of(move):
    return [(flat(*place), flat(*move(*place))) for place in places()]


def along_first(n):
    return perm_of(
        lambda x, y, z, core: (x, (y + n) % 4, z, core) if core == 0 else (x, y, (z + n) % 4, core)
    )


def along_second(n):
    return perm_of(
        lambda x, y, z, core: (x, (y + n) % 4, z, core) if core == 1 else (x, y, (z + n) % 4, core)
    )


RING_PLACE = (
    2, 1, 6, 3, 3, 7, 4, 0, 5, 6, 1, 4, 0, 5, 7, 2, 2, 0, 7, 3, 3, 7, 0, 4, 5, 6, 1, 5, 4, 1, 6, 2,
    5, 7, 0, 4, 1, 5, 2, 6, 3, 0, 6, 2, 7, 3, 4, 1, 4, 7, 0, 4, 5, 0, 2, 6, 3, 1, 6, 2, 7, 3, 1, 5,
    1, 2, 2, 6, 6, 3, 7, 4, 4, 7, 5, 0, 0, 5, 3, 1, 0, 2, 2, 7, 7, 3, 6, 4, 5, 6, 4, 0, 1, 5, 3, 1,
    7, 4, 5, 0, 0, 5, 3, 1, 1, 2, 2, 7, 6, 3, 4, 6, 7, 5, 0, 4, 5, 0, 2, 6, 1, 3, 3, 7, 6, 2, 4, 1,
)


def ring_place(x, y, z, core):
    return divmod(RING_PLACE[((x * 4 + y) * 4 + z) * 2 + core], 2)


def to_readers():
    def move(x, y, z, core):
        to_x, to_core = ring_place(x, y, z, core)
        return to_x, x, 2 * (y // 2) + core, to_core

    return perm_of(move)


def along_x(n):
    return perm_of(lambda x, y, z, core: ((x + n) % 4, y, z, core))


def other_core():
    return perm_of(lambda x, y, z, core: (x, y, z, 1 - core))


def slot_table():
    offsets = (0, -1, 1, 2)
    first_order = [(k, n) for n in (0, 1, -1) for k in range(4)] + [(k, 2) for k in range(4)]
    table = np.zeros((128, 24), np.int32)
    for x, y, z, core in places():
        row = table[flat(x, y, z, core)]
        first, second = (y, z) if core == 0 else (z, y)
        for at, (k, n) in enumerate(first_order):
            pos1, pos2 = (first + offsets[k]) % 4, (second - n) % 4
            ys, zs = (pos1, pos2) if core == 0 else (pos2, pos1)
            row[at] = (2 * ys + zs % 2) * 2 + zs // 2
        held = {
            ring_place(y, ys, zs, z % 2): (zs // 2) * 4 + (ys % 2) * 2 + zs % 2
            for ys in (2 * (z // 2), 2 * (z // 2) + 1)
            for zs in range(4)
        }
        for other in range(2):
            for k in range(4):
                row[16 + other * 4 + k] = held[(x + offsets[k]) % 4, core ^ other]
    return table


def dot_nt(a, b):
    return lax.dot_general(a, b, (((1,), (1,)), ((), ())), preferred_element_type=F32)


def dot_nn(a, b):
    return jnp.dot(a, b, preferred_element_type=F32)


def split3(value):
    hi = value.astype(BF16)
    rest = value - hi.astype(F32)
    mid = rest.astype(BF16)
    return hi, mid, (rest - mid.astype(F32)).astype(BF16)


def mirrored(traces):
    rows = traces.shape[0]
    last = NT % 128 - 1
    lane = lax.broadcasted_iota(jnp.int32, (rows, 128), 1)
    source = jnp.where(lane <= last, last - lane, last + 128 - lane)
    tail = jnp.concatenate([traces[:, NT - last - 1:], traces[:, : 127 - last]], axis=1)
    columns = [tail] + [
        traces[:, 128 * n:128 * n + 128] for n in range(NT // 128 - 1, NT // 128 - 2 - HALF // 128, -1)
    ]
    turned = [jnp.take_along_axis(column, source, axis=1) for column in columns]
    return jnp.concatenate(
        [jnp.where(lane <= last, turned[n], turned[n + 1]) for n in range(HALF // 128)], axis=1
    )


def products(table, value):
    hi, mid, lo = split3(value)
    by_hi = dot_nt(table, hi)
    by_mid = dot_nt(table[: 2 * NF], mid)
    by_lo = dot_nt(table[:NF], lo)
    small = by_hi[2 * NF:] + by_lo + by_mid[NF:]
    return by_hi[:NF] + (by_hi[NF:2 * NF] + by_mid[:NF] + small)


def ones_at(size, place):
    row = lax.broadcasted_iota(jnp.int32, (size, size), 0)
    col = lax.broadcasted_iota(jnp.int32, (size, size), 1)
    return jnp.where(col == place(row), jnp.float32(1), jnp.float32(0)).astype(BF16)


def spectra_kernel(
    alive_ref, traces_ref, table_ref, turn_ref, near_ref, counts_ref, out_ref, total_ref,
):
    step = pl.program_id(0)
    lanes = traces_ref.shape[0] * CH
    traces = traces_ref[...].reshape(lanes, NT)
    front, back = traces[:, :HALF], mirrored(traces)
    even = products(table_ref[: 3 * NF], front + back)
    odd = products(table_ref[3 * NF:], front - back)
    cos, sin = turn_ref[:, 0:1], turn_ref[:, 1:2]
    at = pl.ds(pl.multiple_of(step * lanes, 128), lanes)
    total_ref[:NF, at] = even * cos + odd * sin
    total_ref[NF:, at] = even * sin - odd * cos

    @pl.when(step == pl.num_programs(0) - 1)
    def _():
        real, imag = total_ref[:NF], total_ref[NF:]
        magnitude = jnp.sqrt(real * real + imag * imag)
        m_hi, m_mid, m_lo = split3(magnitude)
        near = near_ref[...]
        smooth = (dot_nn(near, m_lo) + dot_nn(near, m_mid) + dot_nn(near, m_hi)) / counts_ref[...]
        water = jnp.sum(magnitude, axis=0, keepdims=True) * (1.0 / NF)
        weight = 1.0 / (smooth + 0.05 * water + 1e-6)
        white = jnp.concatenate([real * weight, imag * weight], axis=0).astype(BF16)
        by_channel = dot_nn(white, ones_at(512, lambda n: (n % CH) * SEG_DEV + n // CH)).astype(BF16)
        alive = [alive_ref[c].astype(F32) for c in range(CH)]
        lhs = jnp.concatenate(
            [
                jnp.concatenate(
                    [by_channel[g * PAIRS:(g + 1) * PAIRS, 128 * b:128 * b + 128] for g in range(4)],
                    axis=1,
                )
                for b in range(4)
            ],
            axis=0,
        )
        by_pair = ones_at(128, lambda n: (n % CH) * 8 + n // CH)
        grouped = dot_nn(lhs, ones_at(512, lambda n: (n // 32 % 4) * 128 + (n // 128) * 32 + n % 32))
        for half in range(PAIRS // 16):
            cols = []
            for part in range(2):
                at = 16 * half + 8 * part
                cols.append(
                    jnp.concatenate(
                        [
                            grouped[
                                PAIRS * (c // 4) + at:PAIRS * (c // 4) + at + 8,
                                128 * (c % 4):128 * (c % 4) + 128,
                            ]
                            * alive[c]
                            for c in range(CH)
                        ],
                        axis=0,
                    )
                )
            block = jnp.concatenate(cols, axis=1).astype(BF16)
            block = dot_nn(by_pair, block).astype(BF16)
            for part in range(2):
                at = 16 * half + 8 * part
                out_ref[at:at + 8] = block[:, 128 * part:128 * part + 128].reshape(8, CH, 128)


def whitened(traces, alive):
    steps = 2
    near, counts = smoothing_tables()
    consts = forward_tables() + (near, counts)
    whole = lambda a: pl.BlockSpec(a.shape, lambda i: (0,) * a.ndim)
    return pl.pallas_call(
        spectra_kernel,
        grid=(steps,),
        out_shape=jax.ShapeDtypeStruct((PAIRS, CH, 128), BF16),
        in_specs=[
            pl.BlockSpec(memory_space=pltpu.SMEM),
            pl.BlockSpec((SEG_DEV // steps, CH, NT), lambda i: (i, 0, 0)),
        ]
        + [whole(a) for a in consts],
        out_specs=pl.BlockSpec((PAIRS, CH, 128), lambda i: (0, 0, 0)),
        scratch_shapes=[pltpu.VMEM((2 * NF, SEG_DEV * CH), F32)],
        compiler_params=pltpu.CompilerParams(vmem_limit_bytes=VMEM),
        name="whitened_spectra",
    )(alive, traces, *(jnp.asarray(a) for a in consts))


CHUNKS = 3
AHEAD = 2
PER = PAIRS // CHUNKS
J_STEP = 8


def stack_kernel(slots_ref, *refs):
    sources, table_ref, out_ref = refs[:10], refs[10], refs[11]
    left, right, waves = refs[12:15]
    cross_refs, sems, wave_sem = refs[15:19], refs[19], refs[20]
    step = pl.program_id(0)

    def copies(chunk):
        at = pl.ds(chunk * PER, PER)
        found = []
        for ref in sources:
            for k in range(ref.shape[0] if len(ref.shape) == 4 else 1):
                to = left if len(found) < 16 else right
                part = ref.at[k, at] if len(ref.shape) == 4 else ref.at[at]
                found.append((part, to.at[slots_ref[len(found)], at]))
        return [
            pltpu.make_async_copy(src, dst, sems.at[chunk, n])
            for n, (src, dst) in enumerate(found)
        ]

    table_copy = pltpu.make_async_copy(table_ref, waves, wave_sem)

    @pl.when(step == 0)
    def _():
        pending = [copies(chunk) for chunk in range(CHUNKS)]
        for chunk in pending[:AHEAD]:
            for copy in chunk:
                copy.start()
        table_copy.start()
        lane = lax.broadcasted_iota(jnp.int32, (CH, 128), 1)
        even = (lane // 32) % 2 == 0
        one, zero = jnp.float32(1), jnp.float32(0)
        sign = jnp.where(lane < 64, -one, one)
        keep0 = jnp.where(even, one, zero).astype(BF16)
        keep1 = jnp.where(even, zero, one).astype(BF16)
        turn0 = (sign * jnp.where(even, one, zero)).astype(BF16)
        turn1 = (sign * jnp.where(even, zero, one)).astype(BF16)

        def cross(p, _):
            first = jnp.concatenate(
                [jnp.concatenate([left[2 * u + h, p] for u in range(8)], axis=0) for h in range(2)],
                axis=1,
            )
            cols = []
            for h in range(2):
                blocks = [right[4 * h + n, p] for n in range(4)]
                swapped = [jnp.concatenate([b[:, 64:], b[:, :64]], axis=1) for b in blocks]
                cols.append(
                    jnp.concatenate(
                        [b * keep0 for b in blocks]
                        + [b * turn0 for b in swapped]
                        + [b * keep1 for b in blocks]
                        + [b * turn1 for b in swapped],
                        axis=0,
                    )
                )
            product = dot_nt(jnp.concatenate(cols, axis=1), first)
            for g in range(4):
                cross_refs[g][pl.ds(p, 64, stride=XROWS), :] = product[64 * g:64 * g + 64]
            return 0

        for chunk in range(CHUNKS):
            for copy in pending[chunk]:
                copy.wait()
            for late in pending[chunk + AHEAD:chunk + AHEAD + 1]:
                for copy in late:
                    copy.start()
            lax.fori_loop(chunk * PER, (chunk + 1) * PER, cross, 0, unroll=UNROLL)
        table_copy.wait()

    out_rows = out_ref.reshape(LAGS * J_STEP, 128)
    turned = 7 - lax.broadcasted_iota(jnp.int32, (LAG_ROWS // 8, 8, 128), 1)
    for pair in range(J_STEP // 2):
        halves = []
        for reim in range(2):
            cols = []
            for e in range(2):
                j = step * J_STEP + 2 * pair + e
                at = pl.ds(pl.multiple_of(j * XROWS, 8), PAIRS)
                x = [cross_refs[2 * kpar + reim][at, :].astype(BF16) for kpar in range(2)]
                cols.append(jnp.concatenate(x * TERMS, axis=0))
            rows = slice(LAG_ROWS * reim, LAG_ROWS * (reim + 1))
            halves.append(dot_nn(waves[rows, :], jnp.concatenate(cols, axis=1)))
        later, earlier = halves[0] + halves[1], halves[0] - halves[1]
        for e in range(2):
            lanes, j = slice(128 * e, 128 * e + 128), 2 * pair + e
            back = earlier[:, lanes].reshape(LAG_ROWS // 8, 8, 128)
            back = jnp.take_along_axis(back, turned, axis=1)
            for v in range(MAXLAG // 8):
                out_rows[pl.ds((MAXLAG - 7 - 8 * v) * J_STEP + j, 8, stride=J_STEP), :] = back[v]
            out_rows[pl.ds(j, 1), :] = earlier[MAXLAG:MAXLAG + 1, lanes]
            out_rows[pl.ds(MAXLAG * J_STEP + j, MAXLAG + 1, stride=J_STEP), :] = later[: MAXLAG + 1, lanes]


UNROLL = 32


def stacked(slots, sources, table):
    any_spec = pl.BlockSpec(memory_space=pl.ANY)
    return pl.pallas_call(
        stack_kernel,
        grid_spec=pltpu.PrefetchScalarGridSpec(
            num_scalar_prefetch=1,
            grid=(64 // J_STEP,),
            in_specs=[any_spec] * (len(sources) + 1),
            out_specs=pl.BlockSpec((LAGS, J_STEP, 128), lambda u, s: (0, u, 0)),
            scratch_shapes=[
                pltpu.VMEM((16, PAIRS, CH, 128), BF16),
                pltpu.VMEM((8, PAIRS, CH, 128), BF16),
                pltpu.VMEM(table.shape, BF16),
            ]
            + [pltpu.VMEM((64 * XROWS, 128), F32)] * 4
            + [pltpu.SemaphoreType.DMA((CHUNKS, 24)), pltpu.SemaphoreType.DMA],
        ),
        out_shape=jax.ShapeDtypeStruct((LAGS, 64, 128), F32),
        compiler_params=pltpu.CompilerParams(vmem_limit_bytes=VMEM),
        cost_estimate=pl.CostEstimate(
            flops=2 * 10**10, bytes_accessed=24 * 2**20, transcendentals=0
        ),
        name="stacks",
    )(slots, *sources, table)


def body(traces, channel_alive):
    own = whitened(traces, channel_alive)
    device = (lax.axis_index("row") * 8 + lax.axis_index("col")) * 2 + lax.axis_index("seg")
    slots = lax.dynamic_index_in_dim(jnp.asarray(slot_table()), device, 0, keepdims=False)
    send = lambda a, perm: lax.ppermute(a, AXES, perm)
    first = [own] + [send(own, along_first(n)) for n in (1, -1, 2)]
    second = send(own, to_readers())
    *first, second = lax.optimization_barrier((*first, second))
    mine = jnp.stack(first)
    up, down = send(mine, along_second(1)), send(mine, along_second(-1))
    seconds = [second] + [send(second, along_x(n)) for n in (1, -1, 2)]
    up, down, *seconds = lax.optimization_barrier((up, down, *seconds))
    seconds = jnp.stack(seconds)
    far_up, far_down = send(up[:2], along_second(1)), send(down[2:], along_second(-1))
    others = send(seconds, other_core())
    sources = (*first, up, down, far_up, far_down, seconds, others)
    out = stacked(slots, sources, jnp.asarray(inverse_table()))
    return jnp.transpose(out, (2, 1, 0))


def solution(mesh):
    return jax.shard_map(
        body,
        mesh=mesh,
        in_specs=(P("seg", ("row", "col"), None), P(("row", "col"))),
        out_specs=P("row", ("col", "seg"), None),
        check_vma=False,
    )
```

```python
import functools
import math

import jax
import jax.numpy as jnp
import ml_dtypes
import numpy as np
from jax import lax
from jax.experimental import pallas as pl
from jax.experimental.pallas import tpu as pltpu
from jax.sharding import PartitionSpec as P

NT = 2000
NF = 192
F_LO = 8
MAXLAG = 200
LAGS = 2 * MAXLAG + 1
SMOOTH = 5
SEGS = 64
PAIRS = NF // 2
HALF = 1024
CH = 16
SEG_DEV = 32
AXES = ("row", "col", "seg")
XROWS = 104
LAG_ROWS = 208
TERMS = 2
VMEM = 60 * 2**20
BF16 = jnp.bfloat16
F32 = jnp.float32


def split_bf16(table, terms):
    rest = np.asarray(table, np.float64)
    parts = []
    for _ in range(terms):
        part = rest.astype(np.float32).astype(ml_dtypes.bfloat16)
        parts.append(part)
        rest = rest - part.astype(np.float64)
    return np.stack(parts)


def forward_tables():
    times = np.arange(HALF) + 0.5
    window_taper = (0.5 - 0.5 * np.cos(times * (2.0 * np.pi / NT))) * (np.arange(HALF) < NT // 2)
    freqs = F_LO + np.concatenate([2 * np.arange(PAIRS), 2 * np.arange(PAIRS) + 1])
    phase = np.mod(freqs[:, None] * times[None, :], NT) * (2.0 * np.pi / NT)
    waves = [split_bf16(wave * window_taper, 2) for wave in (np.cos(phase), np.sin(phase))]
    table = np.concatenate([wave.reshape(2 * NF, HALF) for wave in waves], axis=0)
    angle = freqs[:, None] * (np.pi / NT)
    turn = np.concatenate([np.cos(angle), np.sin(angle)], axis=1).astype(np.float32)
    return table, turn


def inverse_table():
    shifts = np.arange(LAG_ROWS)
    parts = []
    for reim in range(2):
        cols = []
        for kpar in range(2):
            freqs = F_LO + 2 * np.arange(PAIRS) + kpar
            phase = np.mod(freqs[None, :] * shifts[:, None], NT) * (2.0 * np.pi / NT)
            cols.append(np.cos(phase) if reim == 0 else np.sin(phase))
        table = np.concatenate(cols, axis=1) / math.sqrt(NF * SEGS)
        parts.append(np.concatenate(list(split_bf16(table, TERMS)), axis=1))
    return np.concatenate(parts, axis=0)


def smoothing_tables():
    freqs = np.concatenate([2 * np.arange(PAIRS), 2 * np.arange(PAIRS) + 1])
    near = (np.abs(freqs[:, None] - freqs[None, :]) <= SMOOTH).astype(np.float32)
    return near.astype(ml_dtypes.bfloat16), near.sum(axis=1, keepdims=True)


def flat(x, y, z, core):
    return ((x * 2 + core) * 8 + (y * 2 + z % 2)) * 2 + z // 2


def places():
    return [
        (x, y, z, core)
        for x in range(4) for y in range(4) for z in range(4) for core in range(2)
    ]


def perm_of(move):
    return [(flat(*place), flat(*move(*place))) for place in places()]


def along_first(n):
    return perm_of(
        lambda x, y, z, core: (x, (y + n) % 4, z, core) if core == 0 else (x, y, (z + n) % 4, core)
    )


def along_second(n):
    return perm_of(
        lambda x, y, z, core: (x, (y + n) % 4, z, core) if core == 1 else (x, y, (z + n) % 4, core)
    )


RING_PLACE = (
    2, 1, 6, 3, 3, 7, 4, 0, 5, 6, 1, 4, 0, 5, 7, 2, 2, 0, 7, 3, 3, 7, 0, 4, 5, 6, 1, 5, 4, 1, 6, 2,
    5, 7, 0, 4, 1, 5, 2, 6, 3, 0, 6, 2, 7, 3, 4, 1, 4, 7, 0, 4, 5, 0, 2, 6, 3, 1, 6, 2, 7, 3, 1, 5,
    1, 2, 2, 6, 6, 3, 7, 4, 4, 7, 5, 0, 0, 5, 3, 1, 0, 2, 2, 7, 7, 3, 6, 4, 5, 6, 4, 0, 1, 5, 3, 1,
    7, 4, 5, 0, 0, 5, 3, 1, 1, 2, 2, 7, 6, 3, 4, 6, 7, 5, 0, 4, 5, 0, 2, 6, 1, 3, 3, 7, 6, 2, 4, 1,
)


def ring_place(x, y, z, core):
    return divmod(RING_PLACE[((x * 4 + y) * 4 + z) * 2 + core], 2)


def to_readers():
    def move(x, y, z, core):
        to_x, to_core = ring_place(x, y, z, core)
        return to_x, x, 2 * (y // 2) + core, to_core

    return perm_of(move)


def along_x(n):
    return perm_of(lambda x, y, z, core: ((x + n) % 4, y, z, core))


def other_core():
    return perm_of(lambda x, y, z, core: (x, y, z, 1 - core))


def slot_table():
    offsets = (0, -1, 1, 2)
    first_order = [(k, n) for n in (0, 1, -1) for k in range(4)] + [(k, 2) for k in range(4)]
    table = np.zeros((128, 24), np.int32)
    for x, y, z, core in places():
        row = table[flat(x, y, z, core)]
        first, second = (y, z) if core == 0 else (z, y)
        for at, (k, n) in enumerate(first_order):
            pos1, pos2 = (first + offsets[k]) % 4, (second - n) % 4
            ys, zs = (pos1, pos2) if core == 0 else (pos2, pos1)
            row[at] = (2 * ys + zs % 2) * 2 + zs // 2
        held = {
            ring_place(y, ys, zs, z % 2): (zs // 2) * 4 + (ys % 2) * 2 + zs % 2
            for ys in (2 * (z // 2), 2 * (z // 2) + 1)
            for zs in range(4)
        }
        for other in range(2):
            for k in range(4):
                row[16 + other * 4 + k] = held[(x + offsets[k]) % 4, core ^ other]
    return table


def dot_nt(a, b):
    return lax.dot_general(a, b, (((1,), (1,)), ((), ())), preferred_element_type=F32)


def dot_nn(a, b):
    return jnp.dot(a, b, preferred_element_type=F32)


def split3(value):
    hi = value.astype(BF16)
    rest = value - hi.astype(F32)
    mid = rest.astype(BF16)
    return hi, mid, (rest - mid.astype(F32)).astype(BF16)


def mirrored(traces):
    rows = traces.shape[0]
    last = NT % 128 - 1
    lane = lax.broadcasted_iota(jnp.int32, (rows, 128), 1)
    source = jnp.where(lane <= last, last - lane, last + 128 - lane)
    tail = jnp.concatenate([traces[:, NT - last - 1:], traces[:, : 127 - last]], axis=1)
    columns = [tail] + [
        traces[:, 128 * n:128 * n + 128] for n in range(NT // 128 - 1, NT // 128 - 2 - HALF // 128, -1)
    ]
    turned = [jnp.take_along_axis(column, source, axis=1) for column in columns]
    return jnp.concatenate(
        [jnp.where(lane <= last, turned[n], turned[n + 1]) for n in range(HALF // 128)], axis=1
    )


def products(table, value):
    hi = value.astype(BF16)
    mid = (value - hi.astype(F32)).astype(BF16)
    by_hi = dot_nt(table, hi)
    return by_hi[:NF] + (by_hi[NF:] + dot_nt(table[:NF], mid))


def ones_at(size, place):
    row = lax.broadcasted_iota(jnp.int32, (size, 1), 0)
    col = lax.broadcasted_iota(jnp.int32, (size, size), 1)
    return jnp.where(col == place(row), jnp.float32(1), jnp.float32(0)).astype(BF16)


def spectra_kernel(
    alive_ref, traces_ref, table_ref, turn_ref, near_ref, counts_ref, out_ref, total_ref,
):
    step = pl.program_id(0)
    lanes = traces_ref.shape[0] * CH
    traces = traces_ref[...].reshape(lanes, NT)
    front, back = traces[:, :HALF], mirrored(traces)
    even = products(table_ref[: 2 * NF], front + back)
    odd = products(table_ref[2 * NF:], front - back)
    cos, sin = turn_ref[:, 0:1], turn_ref[:, 1:2]
    at = pl.ds(pl.multiple_of(step * lanes, 128), lanes)
    total_ref[:NF, at] = even * cos + odd * sin
    total_ref[NF:, at] = even * sin - odd * cos

    @pl.when(step == pl.num_programs(0) - 1)
    def _():
        real, imag = total_ref[:NF], total_ref[NF:]
        magnitude = jnp.sqrt(real * real + imag * imag)
        m_hi, m_mid, m_lo = split3(magnitude)
        near = near_ref[...]
        smooth = (dot_nn(near, m_lo) + dot_nn(near, m_mid) + dot_nn(near, m_hi)) / counts_ref[...]
        water = jnp.sum(magnitude, axis=0, keepdims=True) * (1.0 / NF)
        weight = 1.0 / (smooth + 0.05 * water + 1e-6)
        white = jnp.concatenate([real * weight, imag * weight], axis=0).astype(BF16)
        by_channel = dot_nn(white, ones_at(512, lambda n: ((n & 15) << 5) | (n >> 4))).astype(BF16)
        alive = [alive_ref[c].astype(F32) for c in range(CH)]
        lhs = jnp.concatenate(
            [
                jnp.concatenate(
                    [by_channel[g * PAIRS:(g + 1) * PAIRS, 128 * b:128 * b + 128] for g in range(4)],
                    axis=1,
                )
                for b in range(4)
            ],
            axis=0,
        )
        by_pair = ones_at(128, lambda n: ((n & 15) << 3) | (n >> 4))
        grouped = dot_nn(lhs, ones_at(512, lambda n: (((n >> 5) & 3) << 7) | ((n >> 7) << 5) | (n & 31)))
        for half in range(PAIRS // 16):
            cols = []
            for part in range(2):
                at = 16 * half + 8 * part
                cols.append(
                    jnp.concatenate(
                        [
                            grouped[
                                PAIRS * (c // 4) + at:PAIRS * (c // 4) + at + 8,
                                128 * (c % 4):128 * (c % 4) + 128,
                            ]
                            * alive[c]
                            for c in range(CH)
                        ],
                        axis=0,
                    )
                )
            block = jnp.concatenate(cols, axis=1).astype(BF16)
            block = dot_nn(by_pair, block).astype(BF16)
            for part in range(2):
                at = 16 * half + 8 * part
                out_ref[at:at + 8] = block[:, 128 * part:128 * part + 128].reshape(8, CH, 128)


def whitened(traces, alive):
    steps = 2
    near, counts = smoothing_tables()
    consts = forward_tables() + (near, counts)
    whole = lambda a: pl.BlockSpec(a.shape, lambda i: (0,) * a.ndim)
    return pl.pallas_call(
        spectra_kernel,
        grid=(steps,),
        out_shape=jax.ShapeDtypeStruct((PAIRS, CH, 128), BF16),
        in_specs=[
            pl.BlockSpec(memory_space=pltpu.SMEM),
            pl.BlockSpec((SEG_DEV // steps, CH, NT), lambda i: (i, 0, 0)),
        ]
        + [whole(a) for a in consts],
        out_specs=pl.BlockSpec((PAIRS, CH, 128), lambda i: (0, 0, 0)),
        scratch_shapes=[pltpu.VMEM((2 * NF, SEG_DEV * CH), F32)],
        compiler_params=pltpu.CompilerParams(vmem_limit_bytes=VMEM),
        name="whitened_spectra",
    )(alive, traces, *(jnp.asarray(a) for a in consts))


CHUNKS = 3
AHEAD = 2
PER = PAIRS // CHUNKS
J_STEP = 8


def stack_kernel(slots_ref, *refs):
    sources, table_ref, out_ref = refs[:10], refs[10], refs[11]
    left, right, waves = refs[12:15]
    cross_refs, sems, wave_sem = refs[15:19], refs[19], refs[20]
    step = pl.program_id(0)

    def copies(chunk):
        at = pl.ds(chunk * PER, PER)
        found = []
        for ref in sources:
            for k in range(ref.shape[0] if len(ref.shape) == 4 else 1):
                to = left if len(found) < 16 else right
                part = ref.at[k, at] if len(ref.shape) == 4 else ref.at[at]
                found.append((part, to.at[slots_ref[len(found)], at]))
        return [
            pltpu.make_async_copy(src, dst, sems.at[chunk, n])
            for n, (src, dst) in enumerate(found)
        ]

    table_copy = pltpu.make_async_copy(table_ref, waves, wave_sem)

    @pl.when(step == 0)
    def _():
        pending = [copies(chunk) for chunk in range(CHUNKS)]
        for chunk in pending[:AHEAD]:
            for copy in chunk:
                copy.start()
        table_copy.start()
        lane = lax.broadcasted_iota(jnp.int32, (CH, 128), 1)
        even = (lane // 32) % 2 == 0
        one, zero = jnp.float32(1), jnp.float32(0)
        sign = jnp.where(lane < 64, -one, one)
        keep0 = jnp.where(even, one, zero).astype(BF16)
        keep1 = jnp.where(even, zero, one).astype(BF16)
        turn0 = (sign * jnp.where(even, one, zero)).astype(BF16)
        turn1 = (sign * jnp.where(even, zero, one)).astype(BF16)

        def cross(p, _):
            first = jnp.concatenate(
                [jnp.concatenate([left[2 * u + h, p] for u in range(8)], axis=0) for h in range(2)],
                axis=1,
            )
            cols = []
            for h in range(2):
                blocks = [right[4 * h + n, p] for n in range(4)]
                swapped = [jnp.concatenate([b[:, 64:], b[:, :64]], axis=1) for b in blocks]
                cols.append(
                    jnp.concatenate(
                        [b * keep0 for b in blocks]
                        + [b * turn0 for b in swapped]
                        + [b * keep1 for b in blocks]
                        + [b * turn1 for b in swapped],
                        axis=0,
                    )
                )
            product = dot_nt(jnp.concatenate(cols, axis=1), first)
            for g in range(4):
                cross_refs[g][pl.ds(p, 64, stride=XROWS), :] = product[64 * g:64 * g + 64]
            return 0

        for chunk in range(CHUNKS):
            for copy in pending[chunk]:
                copy.wait()
            for late in pending[chunk + AHEAD:chunk + AHEAD + 1]:
                for copy in late:
                    copy.start()
            lax.fori_loop(chunk * PER, (chunk + 1) * PER, cross, 0, unroll=UNROLL)
        table_copy.wait()

    out_rows = out_ref.reshape(LAGS * J_STEP, 128)
    turned = 7 - lax.broadcasted_iota(jnp.int32, (LAG_ROWS // 8, 8, 128), 1)
    for pair in range(J_STEP // 2):
        halves = []
        for reim in range(2):
            cols = []
            for e in range(2):
                j = step * J_STEP + 2 * pair + e
                at = pl.ds(pl.multiple_of(j * XROWS, 8), PAIRS)
                x = [cross_refs[2 * kpar + reim][at, :].astype(BF16) for kpar in range(2)]
                cols.append(jnp.concatenate(x * TERMS, axis=0))
            rows = slice(LAG_ROWS * reim, LAG_ROWS * (reim + 1))
            halves.append(dot_nn(waves[rows, :], jnp.concatenate(cols, axis=1)))
        later, earlier = halves[0] + halves[1], halves[0] - halves[1]
        for e in range(2):
            lanes, j = slice(128 * e, 128 * e + 128), 2 * pair + e
            back = earlier[:, lanes].reshape(LAG_ROWS // 8, 8, 128)
            back = jnp.take_along_axis(back, turned, axis=1)
            for v in range(MAXLAG // 8):
                out_rows[pl.ds((MAXLAG - 7 - 8 * v) * J_STEP + j, 8, stride=J_STEP), :] = back[v]
            out_rows[pl.ds(j, 1), :] = earlier[MAXLAG:MAXLAG + 1, lanes]
            out_rows[pl.ds(MAXLAG * J_STEP + j, MAXLAG + 1, stride=J_STEP), :] = later[: MAXLAG + 1, lanes]


UNROLL = 32


def stacked(slots, sources, table):
    any_spec = pl.BlockSpec(memory_space=pl.ANY)
    return pl.pallas_call(
        stack_kernel,
        grid_spec=pltpu.PrefetchScalarGridSpec(
            num_scalar_prefetch=1,
            grid=(64 // J_STEP,),
            in_specs=[any_spec] * (len(sources) + 1),
            out_specs=pl.BlockSpec((LAGS, J_STEP, 128), lambda u, s: (0, u, 0)),
            scratch_shapes=[
                pltpu.VMEM((16, PAIRS, CH, 128), BF16),
                pltpu.VMEM((8, PAIRS, CH, 128), BF16),
                pltpu.VMEM(table.shape, BF16),
            ]
            + [pltpu.VMEM((64 * XROWS, 128), F32)] * 4
            + [pltpu.SemaphoreType.DMA((CHUNKS, 24)), pltpu.SemaphoreType.DMA],
        ),
        out_shape=jax.ShapeDtypeStruct((LAGS, 64, 128), F32),
        compiler_params=pltpu.CompilerParams(vmem_limit_bytes=VMEM),
        cost_estimate=pl.CostEstimate(
            flops=2 * 10**10, bytes_accessed=24 * 2**20, transcendentals=0
        ),
        name="stacks",
    )(slots, *sources, table)


def body(traces, channel_alive):
    own = whitened(traces, channel_alive)
    device = (lax.axis_index("row") * 8 + lax.axis_index("col")) * 2 + lax.axis_index("seg")
    slots = lax.dynamic_index_in_dim(jnp.asarray(slot_table()), device, 0, keepdims=False)
    send = lambda a, perm: lax.ppermute(a, AXES, perm)
    first = [own] + [send(own, along_first(n)) for n in (1, -1, 2)]
    second = send(own, to_readers())
    *first, second = lax.optimization_barrier((*first, second))
    mine = jnp.stack(first)
    up, down = send(mine, along_second(1)), send(mine, along_second(-1))
    seconds = [second] + [send(second, along_x(n)) for n in (1, -1, 2)]
    up, down, *seconds = lax.optimization_barrier((up, down, *seconds))
    seconds = jnp.stack(seconds)
    far_up, far_down = send(up[:2], along_second(1)), send(down[2:], along_second(-1))
    others = send(seconds, other_core())
    sources = (*first, up, down, far_up, far_down, seconds, others)
    out = stacked(slots, sources, jnp.asarray(inverse_table()))
    return jnp.transpose(out, (2, 1, 0))


def solution(mesh):
    return jax.shard_map(
        body,
        mesh=mesh,
        in_specs=(P("seg", ("row", "col"), None), P(("row", "col"))),
        out_specs=P("row", ("col", "seg"), None),
        check_vma=False,
    )
```

```python
import functools
import math

import jax
import jax.numpy as jnp
import ml_dtypes
import numpy as np
from jax import lax
from jax.experimental import pallas as pl
from jax.experimental.pallas import tpu as pltpu
from jax.sharding import PartitionSpec as P

NT = 2000
NF = 192
F_LO = 8
MAXLAG = 200
LAGS = 2 * MAXLAG + 1
SMOOTH = 5
SEGS = 64
PAIRS = NF // 2
HALF = 1024
CH = 16
SEG_DEV = 32
AXES = ("row", "col", "seg")
XROWS = 104
LAG_ROWS = 208
TERMS = 2
VMEM = 60 * 2**20
BF16 = jnp.bfloat16
F32 = jnp.float32


def split_bf16(table, terms):
    rest = np.asarray(table, np.float64)
    parts = []
    for _ in range(terms):
        part = rest.astype(np.float32).astype(ml_dtypes.bfloat16)
        parts.append(part)
        rest = rest - part.astype(np.float64)
    return np.stack(parts)


def forward_tables():
    times = np.arange(HALF) + 0.5
    window_taper = (0.5 - 0.5 * np.cos(times * (2.0 * np.pi / NT))) * (np.arange(HALF) < NT // 2)
    freqs = F_LO + np.concatenate([2 * np.arange(PAIRS), 2 * np.arange(PAIRS) + 1])
    phase = np.mod(freqs[:, None] * times[None, :], NT) * (2.0 * np.pi / NT)
    waves = [split_bf16(wave * window_taper, 2) for wave in (np.cos(phase), np.sin(phase))]
    table = np.concatenate([wave.reshape(2 * NF, HALF) for wave in waves], axis=0)
    angle = freqs[:, None] * (np.pi / NT)
    turn = np.concatenate([np.cos(angle), np.sin(angle)], axis=1).astype(np.float32)
    return table, turn


def inverse_table():
    shifts = np.arange(LAG_ROWS)
    parts = []
    for reim in range(2):
        cols = []
        for kpar in range(2):
            freqs = F_LO + 2 * np.arange(PAIRS) + kpar
            phase = np.mod(freqs[None, :] * shifts[:, None], NT) * (2.0 * np.pi / NT)
            cols.append(np.cos(phase) if reim == 0 else np.sin(phase))
        table = np.concatenate(cols, axis=1) / math.sqrt(NF * SEGS)
        parts.append(np.concatenate(list(split_bf16(table, TERMS)), axis=1))
    return np.concatenate(parts, axis=0)


def smoothing_tables():
    freqs = np.concatenate([2 * np.arange(PAIRS), 2 * np.arange(PAIRS) + 1])
    near = (np.abs(freqs[:, None] - freqs[None, :]) <= SMOOTH).astype(np.float32)
    return near.astype(ml_dtypes.bfloat16), near.sum(axis=1, keepdims=True)


def flat(x, y, z, core):
    return ((x * 2 + core) * 8 + (y * 2 + z % 2)) * 2 + z // 2


def places():
    return [
        (x, y, z, core)
        for x in range(4) for y in range(4) for z in range(4) for core in range(2)
    ]


def perm_of(move):
    return [(flat(*place), flat(*move(*place))) for place in places()]


def along_first(n):
    return perm_of(
        lambda x, y, z, core: (x, (y + n) % 4, z, core) if core == 0 else (x, y, (z + n) % 4, core)
    )


def along_second(n):
    return perm_of(
        lambda x, y, z, core: (x, (y + n) % 4, z, core) if core == 1 else (x, y, (z + n) % 4, core)
    )


RING_PLACE = (
    2, 1, 6, 3, 3, 7, 4, 0, 5, 6, 1, 4, 0, 5, 7, 2, 2, 0, 7, 3, 3, 7, 0, 4, 5, 6, 1, 5, 4, 1, 6, 2,
    5, 7, 0, 4, 1, 5, 2, 6, 3, 0, 6, 2, 7, 3, 4, 1, 4, 7, 0, 4, 5, 0, 2, 6, 3, 1, 6, 2, 7, 3, 1, 5,
    1, 2, 2, 6, 6, 3, 7, 4, 4, 7, 5, 0, 0, 5, 3, 1, 0, 2, 2, 7, 7, 3, 6, 4, 5, 6, 4, 0, 1, 5, 3, 1,
    7, 4, 5, 0, 0, 5, 3, 1, 1, 2, 2, 7, 6, 3, 4, 6, 7, 5, 0, 4, 5, 0, 2, 6, 1, 3, 3, 7, 6, 2, 4, 1,
)


def ring_place(x, y, z, core):
    return divmod(RING_PLACE[((x * 4 + y) * 4 + z) * 2 + core], 2)


def to_readers():
    def move(x, y, z, core):
        to_x, to_core = ring_place(x, y, z, core)
        return to_x, x, 2 * (y // 2) + core, to_core

    return perm_of(move)


def along_x(n):
    return perm_of(lambda x, y, z, core: ((x + n) % 4, y, z, core))


def other_core():
    return perm_of(lambda x, y, z, core: (x, y, z, 1 - core))


def slot_table():
    offsets = (0, -1, 1, 2)
    first_order = [(k, n) for n in (0, 1, -1) for k in range(4)] + [(k, 2) for k in range(4)]
    table = np.zeros((128, 24), np.int32)
    for x, y, z, core in places():
        row = table[flat(x, y, z, core)]
        first, second = (y, z) if core == 0 else (z, y)
        for at, (k, n) in enumerate(first_order):
            pos1, pos2 = (first + offsets[k]) % 4, (second - n) % 4
            ys, zs = (pos1, pos2) if core == 0 else (pos2, pos1)
            row[at] = (2 * ys + zs % 2) * 2 + zs // 2
        held = {
            ring_place(y, ys, zs, z % 2): (zs // 2) * 4 + (ys % 2) * 2 + zs % 2
            for ys in (2 * (z // 2), 2 * (z // 2) + 1)
            for zs in range(4)
        }
        for other in range(2):
            for k in range(4):
                row[16 + other * 4 + k] = held[(x + offsets[k]) % 4, core ^ other]
    return table


def dot_nt(a, b):
    return lax.dot_general(a, b, (((1,), (1,)), ((), ())), preferred_element_type=F32)


def dot_nn(a, b):
    return jnp.dot(a, b, preferred_element_type=F32)


def split3(value):
    hi = value.astype(BF16)
    rest = value - hi.astype(F32)
    mid = rest.astype(BF16)
    return hi, mid, (rest - mid.astype(F32)).astype(BF16)


def mirrored(traces):
    rows = traces.shape[0]
    last = NT % 128 - 1
    lane = lax.broadcasted_iota(jnp.int32, (rows, 128), 1)
    source = jnp.where(lane <= last, last - lane, last + 128 - lane)
    tail = jnp.concatenate([traces[:, NT - last - 1:], traces[:, : 127 - last]], axis=1)
    columns = [tail] + [
        traces[:, 128 * n:128 * n + 128] for n in range(NT // 128 - 1, NT // 128 - 2 - HALF // 128, -1)
    ]
    turned = [jnp.take_along_axis(column, source, axis=1) for column in columns]
    return jnp.concatenate(
        [jnp.where(lane <= last, turned[n], turned[n + 1]) for n in range(HALF // 128)], axis=1
    )


def products(table, value):
    hi = value.astype(BF16)
    mid = (value - hi.astype(F32)).astype(BF16)
    by_hi = dot_nt(table, hi)
    return by_hi[:NF] + (by_hi[NF:] + dot_nt(table[:NF], mid))


def ones_at(size, place):
    row = lax.broadcasted_iota(jnp.int32, (size, 1), 0)
    col = lax.broadcasted_iota(jnp.int32, (size, size), 1)
    return jnp.where(col == place(row), jnp.float32(1), jnp.float32(0)).astype(BF16)


def spectra_kernel(
    alive_ref, traces_ref, table_ref, turn_ref, near_ref, counts_ref, out_ref, four_ref, total_ref,
):
    step = pl.program_id(0)
    lanes = traces_ref.shape[0] * CH
    traces = traces_ref[...].reshape(lanes, NT)
    front, back = traces[:, :HALF], mirrored(traces)
    even = products(table_ref[: 2 * NF], front + back)
    odd = products(table_ref[2 * NF:], front - back)
    cos, sin = turn_ref[:, 0:1], turn_ref[:, 1:2]
    at = pl.ds(pl.multiple_of(step * lanes, 128), lanes)
    total_ref[:NF, at] = even * cos + odd * sin
    total_ref[NF:, at] = even * sin - odd * cos

    @pl.when(step == pl.num_programs(0) - 1)
    def _():
        real, imag = total_ref[:NF], total_ref[NF:]
        magnitude = jnp.sqrt(real * real + imag * imag)
        m_hi, m_mid, m_lo = split3(magnitude)
        near = near_ref[...]
        smooth = (dot_nn(near, m_lo) + dot_nn(near, m_mid) + dot_nn(near, m_hi)) / counts_ref[...]
        water = jnp.sum(magnitude, axis=0, keepdims=True) * (1.0 / NF)
        weight = 1.0 / (smooth + 0.05 * water + 1e-6)
        white = jnp.concatenate([real * weight, imag * weight], axis=0).astype(BF16)
        by_channel = dot_nn(white, ones_at(512, lambda n: ((n & 15) << 5) | (n >> 4))).astype(BF16)
        alive = [alive_ref[c].astype(F32) for c in range(CH)]
        lhs = jnp.concatenate(
            [
                jnp.concatenate(
                    [by_channel[g * PAIRS:(g + 1) * PAIRS, 128 * b:128 * b + 128] for g in range(4)],
                    axis=1,
                )
                for b in range(4)
            ],
            axis=0,
        )
        by_pair = ones_at(128, lambda n: ((n & 15) << 3) | (n >> 4))
        grouped = dot_nn(lhs, ones_at(512, lambda n: (((n >> 5) & 3) << 7) | ((n >> 7) << 5) | (n & 31)))
        for half in range(PAIRS // 16):
            cols = []
            for part in range(2):
                at = 16 * half + 8 * part
                cols.append(
                    jnp.concatenate(
                        [
                            grouped[
                                PAIRS * (c // 4) + at:PAIRS * (c // 4) + at + 8,
                                128 * (c % 4):128 * (c % 4) + 128,
                            ]
                            * alive[c]
                            for c in range(CH)
                        ],
                        axis=0,
                    )
                )
            block = jnp.concatenate(cols, axis=1).astype(BF16)
            block = dot_nn(by_pair, block).astype(BF16)
            for part in range(2):
                at = 16 * half + 8 * part
                shard = block[:, 128 * part:128 * part + 128].reshape(8, CH, 128)
                out_ref[at:at + 8] = shard
                four_ref[0, at:at + 8] = shard


def whitened(traces, alive):
    steps = 2
    near, counts = smoothing_tables()
    consts = forward_tables() + (near, counts)
    whole = lambda a: pl.BlockSpec(a.shape, lambda i: (0,) * a.ndim)
    return pl.pallas_call(
        spectra_kernel,
        grid=(steps,),
        out_shape=[
            jax.ShapeDtypeStruct((PAIRS, CH, 128), BF16),
            jax.ShapeDtypeStruct((4, PAIRS, CH, 128), BF16),
        ],
        in_specs=[
            pl.BlockSpec(memory_space=pltpu.SMEM),
            pl.BlockSpec((SEG_DEV // steps, CH, NT), lambda i: (i, 0, 0)),
        ]
        + [whole(a) for a in consts],
        out_specs=[
            pl.BlockSpec((PAIRS, CH, 128), lambda i: (0, 0, 0)),
            pl.BlockSpec((1, PAIRS, CH, 128), lambda i: (0, 0, 0, 0)),
        ],
        scratch_shapes=[pltpu.VMEM((2 * NF, SEG_DEV * CH), F32)],
        compiler_params=pltpu.CompilerParams(vmem_limit_bytes=VMEM),
        name="whitened_spectra",
    )(alive, traces, *(jnp.asarray(a) for a in consts))


CHUNKS = 3
AHEAD = 2
PER = PAIRS // CHUNKS
J_STEP = 8


def stack_kernel(slots_ref, *refs):
    sources, table_ref, out_ref = refs[:-11], refs[-11], refs[-10]
    left, right, waves = refs[-9:-6]
    cross_refs, sems, wave_sem = refs[-6:-2], refs[-2], refs[-1]
    step = pl.program_id(0)

    def copies(chunk):
        at = pl.ds(chunk * PER, PER)
        found = []
        for ref in sources:
            for k in range(ref.shape[0]):
                to = left if len(found) < 16 else right
                found.append((ref.at[k, at], to.at[slots_ref[len(found)], at]))
        return [
            pltpu.make_async_copy(src, dst, sems.at[chunk, n])
            for n, (src, dst) in enumerate(found)
        ]

    table_copy = pltpu.make_async_copy(table_ref, waves, wave_sem)

    @pl.when(step == 0)
    def _():
        pending = [copies(chunk) for chunk in range(CHUNKS)]
        for chunk in pending[:AHEAD]:
            for copy in chunk:
                copy.start()
        table_copy.start()
        lane = lax.broadcasted_iota(jnp.int32, (CH, 128), 1)
        even = (lane // 32) % 2 == 0
        one, zero = jnp.float32(1), jnp.float32(0)
        sign = jnp.where(lane < 64, -one, one)
        keep0 = jnp.where(even, one, zero).astype(BF16)
        keep1 = jnp.where(even, zero, one).astype(BF16)
        turn0 = (sign * jnp.where(even, one, zero)).astype(BF16)
        turn1 = (sign * jnp.where(even, zero, one)).astype(BF16)

        def cross(p, _):
            first = jnp.concatenate(
                [jnp.concatenate([left[2 * u + h, p] for u in range(8)], axis=0) for h in range(2)],
                axis=1,
            )
            cols = []
            for h in range(2):
                blocks = [right[4 * h + n, p] for n in range(4)]
                swapped = [jnp.concatenate([b[:, 64:], b[:, :64]], axis=1) for b in blocks]
                cols.append(
                    jnp.concatenate(
                        [b * keep0 for b in blocks]
                        + [b * turn0 for b in swapped]
                        + [b * keep1 for b in blocks]
                        + [b * turn1 for b in swapped],
                        axis=0,
                    )
                )
            product = dot_nt(jnp.concatenate(cols, axis=1), first)
            for g in range(4):
                cross_refs[g][pl.ds(p, 64, stride=XROWS), :] = product[64 * g:64 * g + 64]
            return 0

        for chunk in range(CHUNKS):
            for copy in pending[chunk]:
                copy.wait()
            for late in pending[chunk + AHEAD:chunk + AHEAD + 1]:
                for copy in late:
                    copy.start()
            lax.fori_loop(chunk * PER, (chunk + 1) * PER, cross, 0, unroll=UNROLL)
        table_copy.wait()

    out_rows = out_ref.reshape(LAGS * J_STEP, 128)
    turned = 7 - lax.broadcasted_iota(jnp.int32, (LAG_ROWS // 8, 8, 128), 1)
    for pair in range(J_STEP // 2):
        halves = []
        for reim in range(2):
            cols = []
            for e in range(2):
                j = step * J_STEP + 2 * pair + e
                at = pl.ds(pl.multiple_of(j * XROWS, 8), PAIRS)
                x = [cross_refs[2 * kpar + reim][at, :].astype(BF16) for kpar in range(2)]
                cols.append(jnp.concatenate(x * TERMS, axis=0))
            rows = slice(LAG_ROWS * reim, LAG_ROWS * (reim + 1))
            halves.append(dot_nn(waves[rows, :], jnp.concatenate(cols, axis=1)))
        later, earlier = halves[0] + halves[1], halves[0] - halves[1]
        for e in range(2):
            lanes, j = slice(128 * e, 128 * e + 128), 2 * pair + e
            back = earlier[:, lanes].reshape(LAG_ROWS // 8, 8, 128)
            back = jnp.take_along_axis(back, turned, axis=1)
            for v in range(MAXLAG // 8):
                out_rows[pl.ds((MAXLAG - 7 - 8 * v) * J_STEP + j, 8, stride=J_STEP), :] = back[v]
            out_rows[pl.ds(j, 1), :] = earlier[MAXLAG:MAXLAG + 1, lanes]
            out_rows[pl.ds(MAXLAG * J_STEP + j, MAXLAG + 1, stride=J_STEP), :] = later[: MAXLAG + 1, lanes]


UNROLL = 32


def stacked(slots, sources, table):
    any_spec = pl.BlockSpec(memory_space=pl.ANY)
    return pl.pallas_call(
        stack_kernel,
        grid_spec=pltpu.PrefetchScalarGridSpec(
            num_scalar_prefetch=1,
            grid=(64 // J_STEP,),
            in_specs=[any_spec] * (len(sources) + 1),
            out_specs=pl.BlockSpec((LAGS, J_STEP, 128), lambda u, s: (0, u, 0)),
            scratch_shapes=[
                pltpu.VMEM((16, PAIRS, CH, 128), BF16),
                pltpu.VMEM((8, PAIRS, CH, 128), BF16),
                pltpu.VMEM(table.shape, BF16),
            ]
            + [pltpu.VMEM((64 * XROWS, 128), F32)] * 4
            + [pltpu.SemaphoreType.DMA((CHUNKS, 24)), pltpu.SemaphoreType.DMA],
        ),
        out_shape=jax.ShapeDtypeStruct((LAGS, 64, 128), F32),
        compiler_params=pltpu.CompilerParams(vmem_limit_bytes=VMEM),
        cost_estimate=pl.CostEstimate(
            flops=2 * 10**10, bytes_accessed=24 * 2**20, transcendentals=0
        ),
        name="stacks",
    )(slots, *sources, table)


def body(traces, channel_alive):
    own, mine = whitened(traces, channel_alive)
    device = (lax.axis_index("row") * 8 + lax.axis_index("col")) * 2 + lax.axis_index("seg")
    slots = lax.dynamic_index_in_dim(jnp.asarray(slot_table()), device, 0, keepdims=False)
    send = lambda a, perm: lax.ppermute(a, AXES, perm)
    second = send(own, to_readers())
    for k, n in enumerate((1, -1, 2)):
        mine = lax.dynamic_update_slice(mine, send(own, along_first(n))[None], (k + 1, 0, 0, 0))
    mine, second = lax.optimization_barrier((mine, second))
    up, down = send(mine, along_second(1)), send(mine, along_second(-1))
    seconds = [second] + [send(second, along_x(n)) for n in (1, -1, 2)]
    up, down, *seconds = lax.optimization_barrier((up, down, *seconds))
    seconds = jnp.stack(seconds)
    far_up, far_down = send(up[:2], along_second(1)), send(down[2:], along_second(-1))
    others = send(seconds, other_core())
    sources = (mine, up, down, far_up, far_down, seconds, others)
    out = stacked(slots, sources, jnp.asarray(inverse_table()))
    return jnp.transpose(out, (2, 1, 0))


def solution(mesh):
    return jax.shard_map(
        body,
        mesh=mesh,
        in_specs=(P("seg", ("row", "col"), None), P(("row", "col"))),
        out_specs=P("row", ("col", "seg"), None),
        check_vma=False,
    )
```

```python
import functools
import math

import jax
import jax.numpy as jnp
import ml_dtypes
import numpy as np
from jax import lax
from jax.experimental import pallas as pl
from jax.experimental.pallas import tpu as pltpu
from jax.sharding import PartitionSpec as P

NT = 2000
NF = 192
F_LO = 8
MAXLAG = 200
LAGS = 2 * MAXLAG + 1
SMOOTH = 5
SEGS = 64
PAIRS = NF // 2
HALF = 1024
CH = 16
SEG_DEV = 32
AXES = ("row", "col", "seg")
XROWS = 104
LAG_ROWS = 208
TERMS = 2
VMEM = 60 * 2**20
BF16 = jnp.bfloat16
F32 = jnp.float32


def split_bf16(table, terms):
    rest = np.asarray(table, np.float64)
    parts = []
    for _ in range(terms):
        part = rest.astype(np.float32).astype(ml_dtypes.bfloat16)
        parts.append(part)
        rest = rest - part.astype(np.float64)
    return np.stack(parts)


def forward_tables():
    times = np.arange(HALF) + 0.5
    window_taper = (0.5 - 0.5 * np.cos(times * (2.0 * np.pi / NT))) * (np.arange(HALF) < NT // 2)
    freqs = F_LO + np.concatenate([2 * np.arange(PAIRS), 2 * np.arange(PAIRS) + 1])
    phase = np.mod(freqs[:, None] * times[None, :], NT) * (2.0 * np.pi / NT)
    waves = [split_bf16(wave * window_taper, 2) for wave in (np.cos(phase), np.sin(phase))]
    table = np.concatenate([wave.reshape(2 * NF, HALF) for wave in waves], axis=0)
    angle = freqs[:, None] * (np.pi / NT)
    turn = np.concatenate([np.cos(angle), np.sin(angle)], axis=1).astype(np.float32)
    return table, turn


def inverse_table():
    shifts = np.arange(LAG_ROWS)
    parts = []
    for reim in range(2):
        cols = []
        for kpar in range(2):
            freqs = F_LO + 2 * np.arange(PAIRS) + kpar
            phase = np.mod(freqs[None, :] * shifts[:, None], NT) * (2.0 * np.pi / NT)
            cols.append(np.cos(phase) if reim == 0 else np.sin(phase))
        table = np.concatenate(cols, axis=1) / math.sqrt(NF * SEGS)
        parts.append(np.concatenate(list(split_bf16(table, TERMS)), axis=1))
    return np.concatenate(parts, axis=0)


def smoothing_tables():
    freqs = np.concatenate([2 * np.arange(PAIRS), 2 * np.arange(PAIRS) + 1])
    near = (np.abs(freqs[:, None] - freqs[None, :]) <= SMOOTH).astype(np.float32)
    return near.astype(ml_dtypes.bfloat16), near.sum(axis=1, keepdims=True)


def flat(x, y, z, core):
    return ((x * 2 + core) * 8 + (y * 2 + z % 2)) * 2 + z // 2


def places():
    return [
        (x, y, z, core)
        for x in range(4) for y in range(4) for z in range(4) for core in range(2)
    ]


def perm_of(move):
    return [(flat(*place), flat(*move(*place))) for place in places()]


def along_first(n):
    return perm_of(
        lambda x, y, z, core: (x, (y + n) % 4, z, core) if core == 0 else (x, y, (z + n) % 4, core)
    )


def along_second(n):
    return perm_of(
        lambda x, y, z, core: (x, (y + n) % 4, z, core) if core == 1 else (x, y, (z + n) % 4, core)
    )


RING_PLACE = (
    2, 1, 6, 3, 3, 7, 4, 0, 5, 6, 1, 4, 0, 5, 7, 2, 2, 0, 7, 3, 3, 7, 0, 4, 5, 6, 1, 5, 4, 1, 6, 2,
    5, 7, 0, 4, 1, 5, 2, 6, 3, 0, 6, 2, 7, 3, 4, 1, 4, 7, 0, 4, 5, 0, 2, 6, 3, 1, 6, 2, 7, 3, 1, 5,
    1, 2, 2, 6, 6, 3, 7, 4, 4, 7, 5, 0, 0, 5, 3, 1, 0, 2, 2, 7, 7, 3, 6, 4, 5, 6, 4, 0, 1, 5, 3, 1,
    7, 4, 5, 0, 0, 5, 3, 1, 1, 2, 2, 7, 6, 3, 4, 6, 7, 5, 0, 4, 5, 0, 2, 6, 1, 3, 3, 7, 6, 2, 4, 1,
)


def ring_place(x, y, z, core):
    return divmod(RING_PLACE[((x * 4 + y) * 4 + z) * 2 + core], 2)


def to_readers():
    def move(x, y, z, core):
        to_x, to_core = ring_place(x, y, z, core)
        return to_x, x, 2 * (y // 2) + core, to_core

    return perm_of(move)


def along_x(n):
    return perm_of(lambda x, y, z, core: ((x + n) % 4, y, z, core))


def other_core():
    return perm_of(lambda x, y, z, core: (x, y, z, 1 - core))


def slot_table():
    offsets = (0, -1, 1, 2)
    first_order = [(k, n) for n in (0, 1, -1) for k in range(4)] + [(k, 2) for k in range(4)]
    table = np.zeros((128, 24), np.int32)
    for x, y, z, core in places():
        row = table[flat(x, y, z, core)]
        first, second = (y, z) if core == 0 else (z, y)
        for at, (k, n) in enumerate(first_order):
            pos1, pos2 = (first + offsets[k]) % 4, (second - n) % 4
            ys, zs = (pos1, pos2) if core == 0 else (pos2, pos1)
            row[at] = (2 * ys + zs % 2) * 2 + zs // 2
        held = {
            ring_place(y, ys, zs, z % 2): (zs // 2) * 4 + (ys % 2) * 2 + zs % 2
            for ys in (2 * (z // 2), 2 * (z // 2) + 1)
            for zs in range(4)
        }
        for other in range(2):
            for k in range(4):
                row[16 + other * 4 + k] = held[(x + offsets[k]) % 4, core ^ other]
    return table


def dot_nt(a, b):
    return lax.dot_general(a, b, (((1,), (1,)), ((), ())), preferred_element_type=F32)


def dot_nn(a, b):
    return jnp.dot(a, b, preferred_element_type=F32)


def split3(value):
    hi = value.astype(BF16)
    rest = value - hi.astype(F32)
    mid = rest.astype(BF16)
    return hi, mid, (rest - mid.astype(F32)).astype(BF16)


def mirrored(traces):
    rows = traces.shape[0]
    last = NT % 128 - 1
    lane = lax.broadcasted_iota(jnp.int32, (rows, 128), 1)
    source = jnp.where(lane <= last, last - lane, last + 128 - lane)
    tail = jnp.concatenate([traces[:, NT - last - 1:], traces[:, : 127 - last]], axis=1)
    columns = [tail] + [
        traces[:, 128 * n:128 * n + 128] for n in range(NT // 128 - 1, NT // 128 - 2 - HALF // 128, -1)
    ]
    turned = [jnp.take_along_axis(column, source, axis=1) for column in columns]
    return jnp.concatenate(
        [jnp.where(lane <= last, turned[n], turned[n + 1]) for n in range(HALF // 128)], axis=1
    )


def products(table, value):
    hi = value.astype(BF16)
    mid = (value - hi.astype(F32)).astype(BF16)
    by_hi = dot_nt(table, hi)
    return by_hi[:NF] + (by_hi[NF:] + dot_nt(table[:NF], mid))


def ones_at(size, place):
    row = lax.broadcasted_iota(jnp.int32, (size, 1), 0)
    col = lax.broadcasted_iota(jnp.int32, (size, size), 1)
    return jnp.where(col == place(row), jnp.float32(1), jnp.float32(0)).astype(BF16)


def spectra_kernel(
    alive_ref, traces_ref, table_ref, turn_ref, near_ref, counts_ref, out_ref, four_ref, total_ref,
):
    step = pl.program_id(0)
    lanes = traces_ref.shape[0] * CH
    traces = traces_ref[...].reshape(lanes, NT)
    front, back = traces[:, :HALF], mirrored(traces)
    even = products(table_ref[: 2 * NF], front + back)
    odd = products(table_ref[2 * NF:], front - back)
    cos, sin = turn_ref[:, 0:1], turn_ref[:, 1:2]
    at = pl.ds(pl.multiple_of(step * lanes, 128), lanes)
    total_ref[:NF, at] = even * cos + odd * sin
    total_ref[NF:, at] = even * sin - odd * cos

    @pl.when(step == pl.num_programs(0) - 1)
    def _():
        real, imag = total_ref[:NF], total_ref[NF:]
        magnitude = jnp.sqrt(real * real + imag * imag)
        m_hi, m_mid, m_lo = split3(magnitude)
        near = near_ref[...]
        smooth = (dot_nn(near, m_lo) + dot_nn(near, m_mid) + dot_nn(near, m_hi)) / counts_ref[...]
        water = jnp.sum(magnitude, axis=0, keepdims=True) * (1.0 / NF)
        weight = 1.0 / (smooth + 0.05 * water + 1e-6)
        white = jnp.concatenate([real * weight, imag * weight], axis=0).astype(BF16)
        by_channel = dot_nn(white, ones_at(512, lambda n: ((n & 15) << 5) | (n >> 4))).astype(BF16)
        alive = [alive_ref[c].astype(F32) for c in range(CH)]
        lhs = jnp.concatenate(
            [
                jnp.concatenate(
                    [by_channel[g * PAIRS:(g + 1) * PAIRS, 128 * b:128 * b + 128] for g in range(4)],
                    axis=1,
                )
                for b in range(4)
            ],
            axis=0,
        )
        by_pair = ones_at(128, lambda n: ((n & 15) << 3) | (n >> 4))
        grouped = dot_nn(lhs, ones_at(512, lambda n: (((n >> 5) & 3) << 7) | ((n >> 7) << 5) | (n & 31)))
        for half in range(PAIRS // 16):
            cols = []
            for part in range(2):
                at = 16 * half + 8 * part
                cols.append(
                    jnp.concatenate(
                        [
                            grouped[
                                PAIRS * (c // 4) + at:PAIRS * (c // 4) + at + 8,
                                128 * (c % 4):128 * (c % 4) + 128,
                            ]
                            * alive[c]
                            for c in range(CH)
                        ],
                        axis=0,
                    )
                )
            block = jnp.concatenate(cols, axis=1).astype(BF16)
            block = dot_nn(by_pair, block).astype(BF16)
            for part in range(2):
                at = 16 * half + 8 * part
                shard = block[:, 128 * part:128 * part + 128].reshape(8, CH, 128)
                out_ref[at:at + 8] = shard
                four_ref[0, at:at + 8] = shard


def whitened(traces, alive):
    steps = 2
    near, counts = smoothing_tables()
    consts = forward_tables() + (near, counts)
    whole = lambda a: pl.BlockSpec(a.shape, lambda i: (0,) * a.ndim)
    return pl.pallas_call(
        spectra_kernel,
        grid=(steps,),
        out_shape=[
            jax.ShapeDtypeStruct((PAIRS, CH, 128), BF16),
            jax.ShapeDtypeStruct((4, PAIRS, CH, 128), BF16),
        ],
        in_specs=[
            pl.BlockSpec(memory_space=pltpu.SMEM),
            pl.BlockSpec((SEG_DEV // steps, CH, NT), lambda i: (i, 0, 0)),
        ]
        + [whole(a) for a in consts],
        out_specs=[
            pl.BlockSpec((PAIRS, CH, 128), lambda i: (0, 0, 0)),
            pl.BlockSpec((1, PAIRS, CH, 128), lambda i: (0, 0, 0, 0)),
        ],
        scratch_shapes=[pltpu.VMEM((2 * NF, SEG_DEV * CH), F32)],
        compiler_params=pltpu.CompilerParams(vmem_limit_bytes=VMEM),
        name="whitened_spectra",
    )(alive, traces, *(jnp.asarray(a) for a in consts))


CHUNKS = 3
AHEAD = 2
PER = PAIRS // CHUNKS
J_STEP = 8


def stack_kernel(slots_ref, *refs):
    sources, table_ref, out_ref = refs[:-11], refs[-11], refs[-10]
    left, right, waves = refs[-9:-6]
    cross_refs, sems, wave_sem = refs[-6:-2], refs[-2], refs[-1]
    step = pl.program_id(0)

    def copies(chunk):
        at = pl.ds(chunk * PER, PER)
        found = []
        for ref in sources:
            for k in range(ref.shape[0]):
                to = left if len(found) < 16 else right
                found.append((ref.at[k, at], to.at[slots_ref[len(found)], at]))
        return [
            pltpu.make_async_copy(src, dst, sems.at[chunk, n])
            for n, (src, dst) in enumerate(found)
        ]

    table_copy = pltpu.make_async_copy(table_ref, waves, wave_sem)

    @pl.when(step == 0)
    def _():
        pending = [copies(chunk) for chunk in range(CHUNKS)]
        for chunk in pending[:AHEAD]:
            for copy in chunk:
                copy.start()
        table_copy.start()
        lane = lax.broadcasted_iota(jnp.int32, (CH, 128), 1)
        even = (lane // 32) % 2 == 0
        one, zero = jnp.float32(1), jnp.float32(0)
        sign = jnp.where(lane < 64, -one, one)
        keep0 = jnp.where(even, one, zero).astype(BF16)
        keep1 = jnp.where(even, zero, one).astype(BF16)
        turn0 = (sign * jnp.where(even, one, zero)).astype(BF16)
        turn1 = (sign * jnp.where(even, zero, one)).astype(BF16)

        def cross(p, _):
            first = jnp.concatenate(
                [jnp.concatenate([left[2 * u + h, p] for u in range(8)], axis=0) for h in range(2)],
                axis=1,
            )
            cols = []
            for h in range(2):
                blocks = [right[4 * h + n, p] for n in range(4)]
                swapped = [jnp.concatenate([b[:, 64:], b[:, :64]], axis=1) for b in blocks]
                cols.append(
                    jnp.concatenate(
                        [b * keep0 for b in blocks]
                        + [b * turn0 for b in swapped]
                        + [b * keep1 for b in blocks]
                        + [b * turn1 for b in swapped],
                        axis=0,
                    )
                )
            product = dot_nt(jnp.concatenate(cols, axis=1), first)
            for g in range(4):
                cross_refs[g][pl.ds(p, 64, stride=XROWS), :] = product[64 * g:64 * g + 64]
            return 0

        for chunk in range(CHUNKS):
            for copy in pending[chunk]:
                copy.wait()
            for late in pending[chunk + AHEAD:chunk + AHEAD + 1]:
                for copy in late:
                    copy.start()
            lax.fori_loop(chunk * PER, (chunk + 1) * PER, cross, 0, unroll=UNROLL)
        table_copy.wait()

    out_rows = out_ref.reshape(LAGS * J_STEP, 128)
    turned = 7 - lax.broadcasted_iota(jnp.int32, (LAG_ROWS // 8, 8, 128), 1)
    for pair in range(J_STEP // 2):
        halves = []
        for reim in range(2):
            cols = []
            for e in range(2):
                j = step * J_STEP + 2 * pair + e
                at = pl.ds(pl.multiple_of(j * XROWS, 8), PAIRS)
                x = [cross_refs[2 * kpar + reim][at, :].astype(BF16) for kpar in range(2)]
                cols.append(jnp.concatenate(x * TERMS, axis=0))
            rows = slice(LAG_ROWS * reim, LAG_ROWS * (reim + 1))
            halves.append(dot_nn(waves[rows, :], jnp.concatenate(cols, axis=1)))
        later, earlier = halves[0] + halves[1], halves[0] - halves[1]
        for e in range(2):
            lanes, j = slice(128 * e, 128 * e + 128), 2 * pair + e
            back = earlier[:, lanes].reshape(LAG_ROWS // 8, 8, 128)
            back = jnp.take_along_axis(back, turned, axis=1)
            for v in range(MAXLAG // 8):
                out_rows[pl.ds((MAXLAG - 7 - 8 * v) * J_STEP + j, 8, stride=J_STEP), :] = back[v]
            out_rows[pl.ds(j, 1), :] = earlier[MAXLAG:MAXLAG + 1, lanes]
            out_rows[pl.ds(MAXLAG * J_STEP + j, MAXLAG + 1, stride=J_STEP), :] = later[: MAXLAG + 1, lanes]


UNROLL = 32


def stacked(slots, sources, table):
    any_spec = pl.BlockSpec(memory_space=pl.ANY)
    return pl.pallas_call(
        stack_kernel,
        grid_spec=pltpu.PrefetchScalarGridSpec(
            num_scalar_prefetch=1,
            grid=(64 // J_STEP,),
            in_specs=[any_spec] * (len(sources) + 1),
            out_specs=pl.BlockSpec((LAGS, J_STEP, 128), lambda u, s: (0, u, 0)),
            scratch_shapes=[
                pltpu.VMEM((16, PAIRS, CH, 128), BF16),
                pltpu.VMEM((8, PAIRS, CH, 128), BF16),
                pltpu.VMEM(table.shape, BF16),
            ]
            + [pltpu.VMEM((64 * XROWS, 128), F32)] * 4
            + [pltpu.SemaphoreType.DMA((CHUNKS, 24)), pltpu.SemaphoreType.DMA],
        ),
        out_shape=jax.ShapeDtypeStruct((LAGS, 64, 128), F32),
        compiler_params=pltpu.CompilerParams(vmem_limit_bytes=VMEM),
        cost_estimate=pl.CostEstimate(
            flops=2 * 10**10, bytes_accessed=24 * 2**20, transcendentals=0
        ),
        name="stacks",
    )(slots, *sources, table)


def body(traces, channel_alive):
    own, mine = whitened(traces, channel_alive)
    device = (lax.axis_index("row") * 8 + lax.axis_index("col")) * 2 + lax.axis_index("seg")
    slots = lax.dynamic_index_in_dim(jnp.asarray(slot_table()), device, 0, keepdims=False)
    send = lambda a, perm: lax.ppermute(a, AXES, perm)
    second = send(own, to_readers())
    for k, n in enumerate((1, -1, 2)):
        mine = lax.dynamic_update_slice(mine, send(own, along_first(n))[None], (k + 1, 0, 0, 0))
    mine, second = lax.optimization_barrier((mine, second))
    up, down = send(mine, along_second(1)), send(mine, along_second(-1))
    seconds = [second] + [send(second, along_x(n)) for n in (1, -1, 2)]
    up, down = lax.optimization_barrier((up, down))
    far_up, far_down = send(up[:2], along_second(1)), send(down[2:], along_second(-1))
    *seconds, up = lax.optimization_barrier((*seconds, up))
    seconds = jnp.stack(seconds)
    others = send(seconds, other_core())
    sources = (mine, up, down, far_up, far_down, seconds, others)
    out = stacked(slots, sources, jnp.asarray(inverse_table()))
    return jnp.transpose(out, (2, 1, 0))


def solution(mesh):
    return jax.shard_map(
        body,
        mesh=mesh,
        in_specs=(P("seg", ("row", "col"), None), P(("row", "col"))),
        out_specs=P("row", ("col", "seg"), None),
        check_vma=False,
    )
```
